128 devices in a mesh: ax: 16 (over z, y_lo, core), rad: 8 (over x, y_hi).
Axes of the slice: x: 4, y: 4 (y_hi: 2, y_lo: 2; y = y_hi * 2 + y_lo), z: 4, core: 2. Of those that a mesh axis runs over, the one named last changes fastest.
Arguments:
- velocity: float32 [3, 128, 512, 1024], P(None, 'ax', 'rad'), may hold values from -6 to 6
- viscosity: float32 [128, 512, 1024], P('ax', 'rad'), may hold values from 0.05 to 0.5
- inv_dx: float32 [128], P('ax'), may hold values from 0.5 to 2
- inv_dr: float32 [512], P('rad'), may hold values from 0.5 to 2
- inv_rt: float32 [512], P('rad'), may hold values from 0.5 to 2
- az_inverse: float32 [1024, 1024], replicated, may hold values from -0.5 to 2.5
- rad_inverse: float32 [512, 512], replicated, may hold values from -0.5 to 2.5
Outputs:
- velocity_next: float32 [3, 128, 512, 1024], P(None, 'ax', 'rad')
The draws below stay inside these ranges and needn't reach their ends.
All inputs are finite; a program needn't handle non-finite values.
Results may differ from the reference program's by a relative error of at most 0.0003.
Values sent between devices are 32-bit elements; how exact they have to be, the bound alone decides.
No kernel may reach another device: no remote copies, remote signals or barrier semaphores. Data moves between devices by JAX's collectives and lax.ppermute only.
A program may use at most 256 MiB of HBM per device.

```python
import math
import jax
import jax.numpy as jnp
from jax import lax

CA = 8
NT = 1024
NR = 512
NA = 128


def inverse_table(key, count, length, periodic):
    key_diag, key_off = jax.random.split(jax.random.fold_in(key, 7))
    index = jnp.arange(count)
    dist = jnp.abs(index[:, None] - index[None, :])
    if periodic:
        dist = jnp.minimum(dist, count - dist)
    dist = dist.astype(jnp.float32)
    factor = jax.random.uniform(key_off, (count, count), jnp.float32, -1.0, 3.0)
    diag = jax.random.uniform(key_diag, (count,), jnp.float32, 0.8, 1.2)
    eye = (dist == 0.0).astype(jnp.float32)
    return eye * diag[:, None] + jnp.exp(-dist / length) * factor * (1.0 / length)


def draw_az_inverse(key, part):
    return inverse_table(key, NT, NT / 8.0, True).astype(jnp.float32)


def draw_rad_inverse(key, part):
    return inverse_table(key, NR, NR / 4.0, False).astype(jnp.float32)


def levels(rng, extent, pieces, least, top_value):
    loudness, own = 1.0, jax.random.fold_in(rng, 6)
    for axis_at, blocks in pieces:
        heights = jnp.exp(jax.random.uniform(jax.random.fold_in(own, axis_at), (blocks,), jnp.float32, least / len(pieces), top_value / len(pieces)))
        loudness = loudness * jnp.repeat(heights, extent[axis_at] // blocks).reshape([-1 if axis == axis_at else 1 for axis in range(len(extent))])
    return loudness


def centred(stream_key, extent, width, limit, pieces=(), held_as=jnp.bfloat16):
    drawn = jax.random.normal(stream_key, extent, jnp.float32) * width
    if len(pieces) > 0:
        drawn = levels(stream_key, extent, pieces, -0.22, 0.18) * drawn
    return jnp.clip(drawn, min=-limit, max=limit).astype(held_as)


def setup_inputs(seed: int = 0) -> dict:
    streams_of = jax.random.split(jax.random.key(seed), 8)
    return {
        "velocity": centred(streams_of[0], (3, NA, NR, NT), 1.0, 6.0, ((1, 16), (2, 8)), jnp.float32),
        "viscosity": jnp.clip(jnp.exp(math.log(0.5) - 2.3025851 * jax.random.uniform(streams_of[1], (NA, NR, NT), jnp.float32) ** levels(streams_of[1], (NA, NR, NT), ((0, 16), (1, 8)), -0.2, 0.2)), 0.05, 0.5),
        "inv_dx": jnp.clip(jnp.exp(math.log(2.0) - 1.3862944 * jax.random.uniform(streams_of[2], (NA,), jnp.float32) ** levels(streams_of[2], (NA,), ((0, 16),), -0.2, 0.2)), 0.5, 2.0),
        "inv_dr": jnp.clip(jnp.exp(math.log(2.0) - 1.3862944 * jax.random.uniform(streams_of[3], (NR,), jnp.float32) ** levels(streams_of[3], (NR,), ((0, 8),), -0.2, 0.2)), 0.5, 2.0),
        "inv_rt": jnp.clip(jnp.exp(math.log(2.0) - 1.3862944 * jax.random.uniform(streams_of[4], (NR,), jnp.float32) ** levels(streams_of[4], (NR,), ((0, 8),), -0.2, 0.2)), 0.5, 2.0),
        "az_inverse": draw_az_inverse(jax.random.fold_in(streams_of[7], 71), 0),
        "rad_inverse": draw_rad_inverse(jax.random.fold_in(streams_of[7], 71), 0),
    }


COEF = 0.25


def tendency(padded, inv_dx, inv_dr, inv_rt):
    planes = padded.shape[1] - 4
    radial = padded.shape[2] - 4

    def shifted(step_a, step_r):
        return padded[:, 2 + step_a:2 + step_a + planes, 2 + step_r:2 + step_r + radial, :]

    centre = shifted(0, 0)
    vel = centre[:3]
    visc = centre[3]
    metric_x = inv_dx[:, None, None]
    metric_r = inv_dr[None, :, None]
    metric_t = inv_rt[None, :, None]

    def parts(metric, plus_one, minus_one, plus_two, minus_two):
        deriv = metric * (8.0 * (plus_one[:3] - minus_one[:3]) - (plus_two[:3] - minus_two[:3])) / 12.0
        upper = 0.5 * (visc + plus_one[3]) * (plus_one[:3] - vel)
        lower = 0.5 * (visc + minus_one[3]) * (vel - minus_one[:3])
        return deriv, metric * metric * (upper - lower)

    deriv_x, diff_x = parts(metric_x, shifted(1, 0), shifted(-1, 0), shifted(2, 0), shifted(-2, 0))
    deriv_r, diff_r = parts(metric_r, shifted(0, 1), shifted(0, -1), shifted(0, 2), shifted(0, -2))
    deriv_t, diff_t = parts(metric_t, jnp.roll(centre, -1, axis=3), jnp.roll(centre, 1, axis=3),
                            jnp.roll(centre, -2, axis=3), jnp.roll(centre, 2, axis=3))
    advect = vel[0] * deriv_x + vel[1] * deriv_t + vel[2] * deriv_r
    return vel + COEF * (diff_x + diff_t + diff_r - advect)


def reference(velocity, viscosity, inv_dx, inv_dr, inv_rt, az_inverse, rad_inverse):
    fields = jnp.concatenate([velocity, viscosity[None]], axis=0)
    padded = jnp.pad(fields, ((0, 0), (2, 2), (2, 2), (0, 0)))
    blocks = NA // CA

    def one_block(index):
        start = (index * CA).astype(jnp.int32)
        piece = lax.dynamic_slice_in_dim(padded, start, CA + 4, 1)
        metric = lax.dynamic_slice_in_dim(inv_dx, start, CA, 0)
        rhs = tendency(piece, metric, inv_dr, inv_rt)
        solved = jnp.einsum('cars,ts->cart', rhs, az_inverse, precision=lax.Precision.HIGHEST)
        return jnp.einsum('rk,cakt->cart', rad_inverse, solved, precision=lax.Precision.HIGHEST)

    result = lax.map(one_block, jnp.arange(blocks, dtype=jnp.int32))
    return result.transpose(1, 0, 2, 3, 4).reshape(3, NA, NR, NT)
```

```python
import functools

import jax
import jax.numpy as jnp
from jax import lax
from jax.experimental import pallas as pl
from jax.experimental.pallas import tpu as pltpu
from jax.sharding import PartitionSpec as P

COEF = 0.25
F32 = jnp.float32
BF16 = jnp.bfloat16
CHUNKS = ((2, 3), (4, 5), (0, 1), (6, 7))
HALF_BYTES = 200 * 1024 * 1024
VMEM_LIMIT = 56 * 1024 * 1024


def split(x):
    hi = x.astype(BF16)
    return hi, (x - hi.astype(F32)).astype(BF16)


def dot3(a_hi, a_lo, b_hi, b_lo, dims):
    dot = functools.partial(
        lax.dot_general, dimension_numbers=(dims, ((), ())), preferred_element_type=F32
    )
    return dot(a_hi, b_hi) + (dot(a_hi, b_lo) + dot(a_lo, b_hi))


def split_kernel(x_ref, hi_ref, lo_ref):
    hi_ref[...], lo_ref[...] = split(x_ref[...])


def split_call(x):
    rows, cols = x.shape
    spec = pl.BlockSpec((256, cols), lambda i: (i, 0))
    return pl.pallas_call(
        split_kernel,
        name=f"split_{rows}",
        grid=(rows // 256,),
        in_specs=[spec],
        out_specs=[spec, spec],
        out_shape=[jax.ShapeDtypeStruct(x.shape, BF16)] * 2,
    )(x)


def rhs_kernel(
    planes, edge, inv_dx, inv_dr, inv_rt, velocity, viscosity, rad_lo, rad_hi, *rest
):
    if edge:
        ax_lo, ax_hi, az_hi, az_lo, out, vbuf, nbuf, rhs, sems = rest
    else:
        az_hi, az_lo, out, vbuf, nbuf, rhs, sems = rest
    rows, nt = velocity.shape[2], velocity.shape[3]
    width = out.shape[3]
    copies = []

    def bring(source, target):
        copy = pltpu.make_async_copy(source, target, sems.at[len(copies)])
        copy.start()
        copies.append(copy)

    for c in range(3):
        bring(velocity.at[c], vbuf.at[c, pl.ds(2, 8), pl.ds(8, rows)])
    bring(viscosity, nbuf.at[pl.ds(2, 8), pl.ds(8, rows)])
    if edge:
        for halo, at, thin in ((ax_lo, 0, 1), (ax_hi, 10, 10)):
            for c in range(3):
                bring(halo.at[pl.ds(2 * c, 2)], vbuf.at[c, pl.ds(at, 2), pl.ds(8, rows)])
            bring(halo.at[6], nbuf.at[thin, pl.ds(8, rows)])
    for copy in copies:
        copy.wait()

    def plane(j, carry):
        p = planes[0] + j
        at = p + 2
        low, high = rad_lo[p], rad_hi[p]
        for c in range(3):
            vbuf[c, at, 0:8, :] = pltpu.roll(low, 6 - 2 * c, 0)
            vbuf[c, at, rows + 8 : rows + 16, :] = pltpu.roll(high, (8 - 2 * c) % 8, 0)
        nbuf[at, 0:8, :] = pltpu.roll(low, 1, 0)
        nbuf[at, rows + 8 : rows + 16, :] = pltpu.roll(high, 2, 0)
        gx = inv_dx[p]

        def strip(i, carry):
            r0 = pl.multiple_of(i * 8, 8)
            mid = pl.ds(pl.multiple_of(r0 + 8, 8), 8)
            wide = pl.ds(r0, 24)
            gr = inv_dr[pl.ds(r0, 8), :]
            gt = inv_rt[pl.ds(r0, 8), :]
            nu = nbuf[at, mid, :]
            nu24 = nbuf[at, wide, :]
            nus = (
                (nbuf[at + 1, mid, :], nbuf[at - 1, mid, :], gx),
                (pltpu.roll(nu, nt - 1, 1), pltpu.roll(nu, 1, 1), gt),
                (nu24[9:17], nu24[7:15], gr),
            )
            coefs = []
            centre = None
            for d, (up, down, g) in enumerate(nus):
                gg = (0.5 * COEF) * g * g
                a_up = gg * (nu + up)
                a_down = gg * (nu + down)
                b = ((COEF / 12.0) * g) * vbuf[d, at, mid, :]
                b8 = 8.0 * b
                total = a_up + a_down
                centre = total if centre is None else centre + total
                coefs.append((a_up - b8, a_down + b8, b))
            centre = 1.0 - centre
            for c in range(3):
                q24 = vbuf[c, at, wide, :]
                q = q24[8:16]
                near = (
                    (
                        vbuf[c, at + 1, mid, :],
                        vbuf[c, at - 1, mid, :],
                        vbuf[c, at + 2, mid, :],
                        vbuf[c, at - 2, mid, :],
                    ),
                    (
                        pltpu.roll(q, nt - 1, 1),
                        pltpu.roll(q, 1, 1),
                        pltpu.roll(q, nt - 2, 1),
                        pltpu.roll(q, 2, 1),
                    ),
                    (q24[9:17], q24[7:15], q24[10:18], q24[6:14]),
                )
                total = centre * q
                for (up, down, up2, down2), (c_up, c_down, b) in zip(near, coefs):
                    total = total + c_up * up + c_down * down + b * (up2 - down2)
                rhs[c, pl.ds(r0, 8), :] = total
            return carry

        lax.fori_loop(0, rows // 8, strip, 0)
        hi, lo = split(rhs[...].reshape(3 * rows, nt))
        solved = dot3(hi, lo, az_hi[...], az_lo[...], ((1,), (1,)))
        for c in range(3):
            for d in range(nt // width):
                out[d, 3 * j + c] = solved[
                    c * rows : (c + 1) * rows, d * width : (d + 1) * width
                ]
        return carry

    lax.fori_loop(0, len(planes), plane, 0)


def rhs_call(planes, parts, inv_dx, inv_dr, inv_rt, velocity, viscosity, rad_lo, rad_hi, ax, az):
    rows, nt = velocity.shape[2], velocity.shape[3]
    anywhere = pl.BlockSpec(memory_space=pl.ANY)
    vmem = pl.BlockSpec(memory_space=pltpu.VMEM)
    slabs = 3 * len(planes)
    return pl.pallas_call(
        functools.partial(rhs_kernel, planes, bool(ax)),
        name=f"rhs_{planes[0]}",
        in_specs=[pl.BlockSpec(memory_space=pltpu.SMEM), vmem, vmem, anywhere, anywhere, vmem, vmem]
        + [anywhere] * len(ax)
        + [vmem, vmem],
        out_specs=vmem,
        out_shape=jax.ShapeDtypeStruct((parts, slabs, rows, nt // parts), F32),
        scratch_shapes=[
            pltpu.VMEM((3, 12, rows + 16, nt), F32),
            pltpu.VMEM((12, rows + 16, nt), F32),
            pltpu.VMEM((3, rows, nt), F32),
            pltpu.SemaphoreType.DMA((12,)),
        ],
        compiler_params=pltpu.CompilerParams(vmem_limit_bytes=VMEM_LIMIT),
        cost_estimate=pl.CostEstimate(
            flops=1024,
            bytes_accessed=1024,
            transcendentals=0,
        ),
    )(inv_dx, inv_dr[:, None], inv_rt[:, None], velocity, viscosity, rad_lo, rad_hi, *ax, *az)


def half_kernel(side_ref, x_ref, hi_ref, lo_ref):
    rows = x_ref.shape[0] // 8
    side = side_ref[0]
    for part in range(4):
        x = x_ref[pl.ds(pl.multiple_of(part * 2 * rows + side * rows, rows), rows), :]
        swapped = jnp.concatenate(
            [
                pltpu.roll(x[:, at : at + 2 * rows], rows, 1)
                for at in range(0, x.shape[1], 2 * rows)
            ],
            axis=1,
        )
        at = slice(part * rows, (part + 1) * rows)
        hi_ref[at, :], lo_ref[at, :] = split(jnp.where(side == 0, x, swapped))


def half_call(side, x):
    rows, cols = x.shape
    vmem = pl.BlockSpec(memory_space=pltpu.VMEM)
    return pl.pallas_call(
        half_kernel,
        name="half",
        in_specs=[pl.BlockSpec(memory_space=pltpu.SMEM), vmem],
        out_specs=[vmem, vmem],
        out_shape=[jax.ShapeDtypeStruct((rows // 2, cols), BF16)] * 2,
        cost_estimate=pl.CostEstimate(
            flops=0, bytes_accessed=HALF_BYTES, transcendentals=0
        ),
    )(side, x)


def radial_kernel(r_hi, r_lo, own_ref, other_ref, out_ref):
    parts, slabs, rows, width = own_ref.shape
    x = jnp.concatenate(
        [
            jnp.concatenate(
                [ref[part, s] for part in range(parts) for ref in (own_ref, other_ref)], axis=0
            )
            for s in range(slabs)
        ],
        axis=1,
    )
    hi, lo = split(x)
    y = dot3(r_hi[...], r_lo[...], hi, lo, ((1,), (0,)))
    for s in range(slabs):
        out_ref[:, s] = y[:, s * width : (s + 1) * width].reshape(parts, rows, width)


def radial_call(rad, own, other):
    parts, slabs, rows, width = own.shape
    step = 3
    block = pl.BlockSpec((parts, step, rows, width), lambda i: (0, i, 0, 0))
    full = pl.BlockSpec(rad[0].shape, lambda i: (0, 0))
    return pl.pallas_call(
        radial_kernel,
        name="radial",
        grid=(slabs // step,),
        in_specs=[full, full, block, block],
        out_specs=block,
        out_shape=jax.ShapeDtypeStruct(own.shape, F32),
        compiler_params=pltpu.CompilerParams(vmem_limit_bytes=VMEM_LIMIT),
        cost_estimate=pl.CostEstimate(
            flops=12 * slabs * parts * rows * parts * rows * width,
            bytes_accessed=12 * own.size,
            transcendentals=0,
        ),
    )(*rad, own, other)


def place_kernel(x_ref, *rest):
    out_ref = rest[-1]
    for d in range(x_ref.shape[0]):
        width = x_ref.shape[3]
        for c in range(x_ref.shape[1]):
            out_ref[c, 0, :, d * width : (d + 1) * width] = x_ref[d, c]


def place_call(planes, x, whole, shape):
    parts, slabs, rows, width = x.shape
    first = planes[0]
    aliased = () if whole is None else (whole,)

    return pl.pallas_call(
        place_kernel,
        name="place",
        grid=(len(planes),),
        in_specs=[pl.BlockSpec((parts, 3, rows, width), lambda j: (0, j, 0, 0))]
        + [pl.BlockSpec(memory_space=pl.ANY)] * len(aliased),
        out_specs=pl.BlockSpec((3, 1, rows, parts * width), lambda j: (0, first + j, 0, 0)),
        out_shape=jax.ShapeDtypeStruct(shape, F32),
        input_output_aliases={1: 0} if aliased else {},
        cost_estimate=pl.CostEstimate(flops=0, bytes_accessed=8 * x.size, transcendentals=0),
    )(x, *aliased)


def pack_kernel(velocity, viscosity, rad_top, rad_bottom, ax_top, ax_bottom, edges, sems):
    planes, rows = viscosity.shape[0], viscosity.shape[1]
    copies = []

    def move(source, target):
        copy = pltpu.make_async_copy(source, target, sems.at[len(copies)])
        copy.start()
        copies.append(copy)

    for side, at in enumerate((rows - 8, 0)):
        for c in range(3):
            move(velocity.at[c, :, pl.ds(at, 8)], edges.at[side, c])
        move(viscosity.at[:, pl.ds(at, 8)], edges.at[side, 3])
    near = len(copies)
    for out, at, thin in ((ax_top, planes - 2, planes - 1), (ax_bottom, 0, 0)):
        for c in range(3):
            move(velocity.at[c, pl.ds(at, 2)], out.at[pl.ds(2 * c, 2)])
        move(viscosity.at[thin], out.at[6])
    for copy in copies[:near]:
        copy.wait()
    row = lax.broadcasted_iota(jnp.int32, edges.shape[3:], 0)
    for p in range(planes):
        for side, out, turns in ((0, rad_top, (2, 4, 6, 7)), (1, rad_bottom, (0, 2, 4, 6))):
            strips = [
                pltpu.roll(edges[side, f, p], turn, 0) if turn else edges[side, f, p]
                for f, turn in enumerate(turns)
            ]
            out[p] = jnp.where(
                row < 4,
                jnp.where(row < 2, strips[0], strips[1]),
                jnp.where(row < 6, strips[2], strips[3]),
            )
    for copy in copies[near:]:
        copy.wait()


def pack_call(velocity, viscosity):
    planes, rows, nt = viscosity.shape
    anywhere = pl.BlockSpec(memory_space=pl.ANY)
    vmem = pl.BlockSpec(memory_space=pltpu.VMEM)
    line = jax.ShapeDtypeStruct((planes, 8, nt), F32)
    face = jax.ShapeDtypeStruct((7, rows, nt), F32)
    return pl.pallas_call(
        pack_kernel,
        name="pack",
        in_specs=[anywhere, anywhere],
        out_specs=[vmem, vmem, vmem, vmem],
        out_shape=[line, line, face, face],
        scratch_shapes=[pltpu.VMEM((2, 4, planes, 8, nt), F32), pltpu.SemaphoreType.DMA((16,))],
        compiler_params=pltpu.CompilerParams(vmem_limit_bytes=VMEM_LIMIT),
    )(velocity, viscosity)


def after(x, *events):
    return lax.optimization_barrier((x, *events))[0]


def local(velocity, viscosity, inv_dx, inv_dr, inv_rt, az_inverse, rad_inverse):
    planes = velocity.shape[1]
    lines = lax.axis_size("rad")
    parts = lines // 2
    side = (lax.axis_index("rad") % 2).astype(jnp.int32).reshape(1)

    def shifts(axis):
        count = lax.axis_size(axis)
        forward = [(i, i + 1) for i in range(count - 1)]
        return forward, [(b, a) for a, b in forward]

    rad_top, rad_bottom, ax_top, ax_bottom = pack_call(velocity, viscosity)
    forward, backward = shifts("rad")
    rad_lo = lax.ppermute(rad_top, "rad", forward)
    rad_hi = lax.ppermute(rad_bottom, "rad", backward)
    forward, backward = shifts("ax")
    ax_top, ax_bottom, rad_lo, rad_hi = lax.optimization_barrier(
        (ax_top, ax_bottom, rad_lo, rad_hi)
    )
    ax_lo = lax.ppermute(ax_top, "ax", forward)
    ax_hi = lax.ppermute(ax_bottom, "ax", backward)

    az = split_call(az_inverse)
    groups = [list(range(0, lines, 2)), list(range(1, lines, 2))]

    def exchange(x):
        return lax.all_to_all(
            x, "rad", split_axis=0, concat_axis=0, tiled=True, axis_index_groups=groups
        )

    def partner(x):
        return lax.ppermute(x, "rad", [(i, i ^ 1) for i in range(lines)])

    count = len(CHUNKS)
    out, own, other, back = [], [], [], []
    for k, chunk in enumerate(CHUNKS):
        edge = min(chunk) < 2 or max(chunk) >= planes - 2
        dx = inv_dx if k == 0 else after(inv_dx, out[-1])
        if k == 2:
            rad = half_call(after(side, ax_lo, ax_hi, out[-1]), rad_inverse)
            dx = after(dx, rad[0])
        if k > 2:
            dx = after(dx, other[k - 3])
        out.append(
            rhs_call(
                chunk, parts, dx, inv_dr, inv_rt, velocity, viscosity, rad_lo, rad_hi,
                (ax_lo, ax_hi) if edge else (), az,
            )
        )
        if k == 1:
            continue
        for j in {0: (0,), 2: (1, 2)}.get(k, (k,)):
            own.append(exchange(after(out[j], own[-1], *((rad[0],) if j == 1 else ())) if j else out[j]))
            if k == 2 and j == 1:
                other.append(partner(after(own[0], rad[0])))
        if k >= 2:
            other.append(partner(after(own[k - 1], rad[0], *((other[k - 3],) if k > 2 else ()))))
    other.append(partner(after(own[count - 1], other[count - 3])))
    whole = None
    for k, chunk in enumerate(CHUNKS):
        solved = radial_call(rad, own[k], other[k])
        back.append(exchange(after(solved, back[-1] if k else own[-1])))
        whole = place_call(chunk, back[k], whole, velocity.shape)
    return whole


def solution(mesh):
    placed = (
        P(None, "ax", "rad", None),
        P("ax", "rad", None),
        P("ax"),
        P("rad"),
        P("rad"),
        P(),
        P(),
    )
    return jax.shard_map(
        local, mesh=mesh, in_specs=placed, out_specs=P(None, "ax", "rad", None), check_vma=False
    )
```

```python
import functools

import jax
import jax.numpy as jnp
from jax import lax
from jax.experimental import pallas as pl
from jax.experimental.pallas import tpu as pltpu
from jax.sharding import PartitionSpec as P

COEF = 0.25
F32 = jnp.float32
BF16 = jnp.bfloat16
CHUNKS = ((2, 3), (4, 5), (0, 1), (6, 7))
RADIAL_BYTES = (8 * 1024 * 1024, 1024, 1024, 1024)
HALF_BYTES = 200 * 1024 * 1024
COLUMNS = 256
VMEM_LIMIT = 56 * 1024 * 1024


def split(x):
    hi = x.astype(BF16)
    return hi, (x - hi.astype(F32)).astype(BF16)


def dot3(a_hi, a_lo, b_hi, b_lo, dims):
    dot = functools.partial(
        lax.dot_general, dimension_numbers=(dims, ((), ())), preferred_element_type=F32
    )
    return dot(a_hi, b_hi) + (dot(a_hi, b_lo) + dot(a_lo, b_hi))


def split_kernel(x_ref, hi_ref, lo_ref):
    hi_ref[...], lo_ref[...] = split(x_ref[...].T)


def split_call(x):
    rows, cols = x.shape
    spec = pl.BlockSpec((256, cols), lambda i: (i, 0))
    return pl.pallas_call(
        split_kernel,
        name=f"split_{rows}",
        grid=(rows // 256,),
        in_specs=[spec],
        out_specs=[pl.BlockSpec((cols, 256), lambda i: (0, i))] * 2,
        out_shape=[jax.ShapeDtypeStruct((cols, rows), BF16)] * 2,
    )(x)


def rhs_kernel(
    groups, edge, inv_dx, inv_dr, inv_rt, velocity, viscosity, rad_lo, rad_hi, *rest
):
    if edge:
        ax_lo, ax_hi, az_hi, az_lo, *outs = rest
    else:
        az_hi, az_lo, *outs = rest
    *outs, vbuf, nbuf, rhs, hi, lo, sems = outs
    planes, rows, nt = viscosity.shape
    width = outs[0].shape[3]
    copies = []

    def bring(source, target):
        copy = pltpu.make_async_copy(source, target, sems.at[len(copies)])
        copy.start()
        copies.append(copy)

    chosen = [p for group in groups for p in group]
    first, last = max(min(chosen) - 2, 0), min(max(chosen) + 3, planes)
    inner, mine = pl.ds(8, rows), pl.ds(first, last - first)
    held = pl.ds(first + 2, last - first)
    for c in range(3):
        bring(velocity.at[c, mine], vbuf.at[c, held, inner])
    bring(viscosity.at[mine], nbuf.at[held, inner])
    if edge:
        for halo, at, thin in ((ax_lo, 0, 1), (ax_hi, planes + 2, planes + 2)):
            for c in range(3):
                bring(halo.at[pl.ds(2 * c, 2)], vbuf.at[c, pl.ds(at, 2), inner])
            bring(halo.at[6], nbuf.at[thin, inner])
    for copy in copies:
        copy.wait()

    def stencil(place, p):
        at = p + 2
        low, high = rad_lo[p], rad_hi[p]
        for c in range(3):
            vbuf[c, at, 0:8, :] = pltpu.roll(low, 6 - 2 * c, 0)
            vbuf[c, at, rows + 8 : rows + 16, :] = pltpu.roll(high, (8 - 2 * c) % 8, 0)
        nbuf[at, 0:8, :] = pltpu.roll(low, 1, 0)
        nbuf[at, rows + 8 : rows + 16, :] = pltpu.roll(high, 2, 0)
        gx = inv_dx[p]

        def strip(i, carry):
            r0 = pl.multiple_of(i * 8, 8)
            mid = pl.ds(pl.multiple_of(r0 + 8, 8), 8)
            wide = pl.ds(r0, 24)
            metrics = (gx, inv_rt[pl.ds(r0, 8), :], inv_dr[pl.ds(r0, 8), :])
            metrics = tuple(
                (g, (0.5 * COEF) * g * g, (COEF / 12.0) * g) for g in metrics
            )
            for l0 in range(0, nt, COLUMNS):
                cols = pl.ds(l0, COLUMNS)
                before, behind = pl.ds((l0 - 128) % nt, 128), pl.ds((l0 + COLUMNS) % nt, 128)

                def turned(ref, *shifts):
                    ext = jnp.concatenate(
                        [ref[mid, before], ref[mid, cols], ref[mid, behind]], axis=1
                    )
                    size = COLUMNS + 256
                    return [
                        pltpu.roll(ext, shift % size, 1)[:, 128 : 128 + COLUMNS]
                        for shift in shifts
                    ]

                nu24 = nbuf[at, wide, cols]
                nu = nu24[8:16]
                nus = (
                    (nbuf[at + 1, mid, cols], nbuf[at - 1, mid, cols]),
                    turned(nbuf.at[at], -1, 1),
                    (nu24[9:17], nu24[7:15]),
                )
                coefs = []
                centre = None
                for d, ((up, down), (_, gg, g12)) in enumerate(zip(nus, metrics)):
                    a_up = gg * (nu + up)
                    a_down = gg * (nu + down)
                    b = g12 * vbuf[d, at, mid, cols]
                    b8 = 8.0 * b
                    total = a_up + a_down
                    centre = total if centre is None else centre + total
                    coefs.append((a_up - b8, a_down + b8, b))
                centre = 1.0 - centre
                for c in range(3):
                    q24 = vbuf[c, at, wide, cols]
                    near = (
                        [vbuf[c, at + k, mid, cols] for k in (1, -1, 2, -2)],
                        turned(vbuf.at[c, at], -1, 1, -2, 2),
                        [q24[8 + k : 16 + k] for k in (1, -1, 2, -2)],
                    )
                    total = centre * q24[8:16]
                    for (up, down, up2, down2), (c_up, c_down, b) in zip(near, coefs):
                        total = total + (c_up * up + c_down * down + b * (up2 - down2))
                    rhs[c, place, pl.ds(r0, 8), cols] = total
            return carry

        lax.fori_loop(0, rows // 8, strip, 0)

    for group, out in zip(groups, outs):
        size = len(group)

        def plane(j, carry):
            stencil(j, group[0] + j)
            return carry

        lax.fori_loop(0, size, plane, 0)
        lines = size * rows
        for c in range(3):
            part = pl.ds(c * lines, lines)
            hi[part, :], lo[part, :] = split(rhs[c, 0:size].reshape(lines, nt))
        for d in range(nt // width):
            cols = pl.ds(d * width, width)
            solved = dot3(
                hi[0 : 3 * lines, :], lo[0 : 3 * lines, :], az_hi[:, cols], az_lo[:, cols],
                ((1,), (0,)),
            )
            out[d] = solved.reshape(3 * size, rows, width)


def rhs_call(groups, parts, inv_dx, inv_dr, inv_rt, velocity, viscosity, rad_lo, rad_hi, ax, az):
    rows, nt = velocity.shape[2], velocity.shape[3]
    anywhere = pl.BlockSpec(memory_space=pl.ANY)
    vmem = pl.BlockSpec(memory_space=pltpu.VMEM)
    most = max(len(group) for group in groups)
    return pl.pallas_call(
        functools.partial(rhs_kernel, groups, bool(ax)),
        name=f"rhs_{groups[0][0]}",
        in_specs=[pl.BlockSpec(memory_space=pltpu.SMEM), vmem, vmem, anywhere, anywhere, vmem, vmem]
        + [anywhere] * len(ax)
        + [vmem, vmem],
        out_specs=[vmem] * len(groups),
        out_shape=[
            jax.ShapeDtypeStruct((parts, 3 * len(group), rows, nt // parts), F32)
            for group in groups
        ],
        scratch_shapes=[
            pltpu.VMEM((3, 12, rows + 16, nt), F32),
            pltpu.VMEM((12, rows + 16, nt), F32),
            pltpu.VMEM((3, most, rows, nt), F32),
            pltpu.VMEM((3 * most * rows, nt), BF16),
            pltpu.VMEM((3 * most * rows, nt), BF16),
            pltpu.SemaphoreType.DMA((12,)),
        ],
        compiler_params=pltpu.CompilerParams(vmem_limit_bytes=VMEM_LIMIT),
        cost_estimate=pl.CostEstimate(flops=1024, bytes_accessed=1024, transcendentals=0),
    )(inv_dx, inv_dr[:, None], inv_rt[:, None], velocity, viscosity, rad_lo, rad_hi, *ax, *az)


def half_kernel(side_ref, x_ref, hi_ref, lo_ref):
    rows = x_ref.shape[0] // 8
    side = side_ref[0]
    for part in range(4):
        x = x_ref[pl.ds(pl.multiple_of(part * 2 * rows + side * rows, rows), rows), :]
        swapped = jnp.concatenate(
            [
                pltpu.roll(x[:, at : at + 2 * rows], rows, 1)
                for at in range(0, x.shape[1], 2 * rows)
            ],
            axis=1,
        )
        at = slice(part * rows, (part + 1) * rows)
        hi_ref[at, :], lo_ref[at, :] = split(jnp.where(side == 0, x, swapped))


def half_call(side, x):
    rows, cols = x.shape
    vmem = pl.BlockSpec(memory_space=pltpu.VMEM)
    return pl.pallas_call(
        half_kernel,
        name="half",
        in_specs=[pl.BlockSpec(memory_space=pltpu.SMEM), vmem],
        out_specs=[vmem, vmem],
        out_shape=[jax.ShapeDtypeStruct((rows // 2, cols), BF16)] * 2,
        cost_estimate=pl.CostEstimate(
            flops=0, bytes_accessed=HALF_BYTES, transcendentals=0
        ),
    )(side, x)


def radial_kernel(r_hi, r_lo, own_ref, other_ref, out_ref):
    parts, slabs, rows, width = own_ref.shape
    x = jnp.concatenate(
        [
            jnp.concatenate(
                [ref[part, s] for part in range(parts) for ref in (own_ref, other_ref)], axis=0
            )
            for s in range(slabs)
        ],
        axis=1,
    )
    hi, lo = split(x)
    y = dot3(r_hi[...], r_lo[...], hi, lo, ((1,), (0,)))
    for s in range(slabs):
        out_ref[:, s] = y[:, s * width : (s + 1) * width].reshape(parts, rows, width)


def radial_call(rad, own, other, moved):
    parts, slabs, rows, width = own.shape
    step = 3
    block = pl.BlockSpec((parts, step, rows, width), lambda i: (0, i, 0, 0))
    full = pl.BlockSpec(rad[0].shape, lambda i: (0, 0))
    return pl.pallas_call(
        radial_kernel,
        name="radial",
        grid=(slabs // step,),
        in_specs=[full, full, block, block],
        out_specs=block,
        out_shape=jax.ShapeDtypeStruct(own.shape, F32),
        compiler_params=pltpu.CompilerParams(vmem_limit_bytes=VMEM_LIMIT),
        cost_estimate=pl.CostEstimate(
            flops=1024,
            bytes_accessed=moved,
            transcendentals=0,
        ),
    )(*rad, own, other)


def place_kernel(x_ref, *rest):
    out_ref = rest[-1]
    parts, width = x_ref.shape[0], x_ref.shape[4]
    for d in range(parts):
        for c in range(3):
            out_ref[c, 0, :, d * width : (d + 1) * width] = x_ref[d, c, 0]


def place_call(planes, x, whole, shape):
    parts, slabs, rows, width = x.shape
    first = planes[0]
    aliased = () if whole is None else (whole,)
    return pl.pallas_call(
        place_kernel,
        name="place",
        grid=(len(planes),),
        in_specs=[pl.BlockSpec((parts, 3, 1, rows, width), lambda j: (0, 0, j, 0, 0))]
        + [pl.BlockSpec(memory_space=pl.ANY)] * len(aliased),
        out_specs=pl.BlockSpec((3, 1, rows, parts * width), lambda j: (0, first + j, 0, 0)),
        out_shape=jax.ShapeDtypeStruct(shape, F32),
        input_output_aliases={1: 0} if aliased else {},
        cost_estimate=pl.CostEstimate(flops=0, bytes_accessed=8 * x.size, transcendentals=0),
    )(x.reshape(parts, 3, slabs // 3, rows, width), *aliased)


def line_kernel(velocity, viscosity, top, bottom, edges, sems):
    planes, rows = viscosity.shape[0], viscosity.shape[1]
    copies = []
    for side, at in enumerate((rows - 8, 0)):
        for f in range(4):
            source = velocity.at[f, :, pl.ds(at, 8)] if f < 3 else viscosity.at[:, pl.ds(at, 8)]
            copies.append(
                pltpu.make_async_copy(source, edges.at[side, f], sems.at[len(copies)])
            )
    for copy in copies:
        copy.start()
    for copy in copies:
        copy.wait()
    row = lax.broadcasted_iota(jnp.int32, edges.shape[3:], 0)
    for p in range(planes):
        for side, out, turns in ((0, top, (2, 4, 6, 7)), (1, bottom, (0, 2, 4, 6))):
            strips = [
                pltpu.roll(edges[side, f, p], turn, 0) if turn else edges[side, f, p]
                for f, turn in enumerate(turns)
            ]
            out[p] = jnp.where(
                row < 4,
                jnp.where(row < 2, strips[0], strips[1]),
                jnp.where(row < 6, strips[2], strips[3]),
            )


def line_call(velocity, viscosity):
    planes, _, nt = viscosity.shape
    anywhere = pl.BlockSpec(memory_space=pl.ANY)
    vmem = pl.BlockSpec(memory_space=pltpu.VMEM)
    return pl.pallas_call(
        line_kernel,
        name="lines",
        in_specs=[anywhere, anywhere],
        out_specs=[vmem, vmem],
        out_shape=[jax.ShapeDtypeStruct((planes, 8, nt), F32)] * 2,
        scratch_shapes=[pltpu.VMEM((2, 4, planes, 8, nt), F32), pltpu.SemaphoreType.DMA((8,))],
        compiler_params=pltpu.CompilerParams(vmem_limit_bytes=VMEM_LIMIT),
    )(velocity, viscosity)


def face_kernel(velocity, viscosity, top, bottom, sems):
    planes = viscosity.shape[0]
    copies = []
    for out, at, thin in ((top, planes - 2, planes - 1), (bottom, 0, 0)):
        for f in range(4):
            source = velocity.at[f, pl.ds(at, 2)] if f < 3 else viscosity.at[pl.ds(thin, 1)]
            target = out.at[pl.ds(2 * f, 2 if f < 3 else 1)]
            copies.append(pltpu.make_async_copy(source, target, sems.at[len(copies)]))
    for copy in copies:
        copy.start()
    for copy in copies:
        copy.wait()


def face_call(velocity, viscosity):
    _, rows, nt = viscosity.shape
    anywhere = pl.BlockSpec(memory_space=pl.ANY)
    vmem = pl.BlockSpec(memory_space=pltpu.VMEM)
    return pl.pallas_call(
        face_kernel,
        name="faces",
        in_specs=[anywhere, anywhere],
        out_specs=[vmem, vmem],
        out_shape=[jax.ShapeDtypeStruct((7, rows, nt), F32)] * 2,
        scratch_shapes=[pltpu.SemaphoreType.DMA((8,))],
        compiler_params=pltpu.CompilerParams(vmem_limit_bytes=VMEM_LIMIT),
    )(velocity, viscosity)


def after(x, *events):
    return lax.optimization_barrier((x, *events))[0]


def local(velocity, viscosity, inv_dx, inv_dr, inv_rt, az_inverse, rad_inverse):
    planes = velocity.shape[1]
    lines = lax.axis_size("rad")
    parts = lines // 2
    side = (lax.axis_index("rad") % 2).astype(jnp.int32).reshape(1)

    def shifts(axis):
        count = lax.axis_size(axis)
        forward = [(i, i + 1) for i in range(count - 1)]
        return forward, [(b, a) for a, b in forward]

    rad_top, rad_bottom = line_call(velocity, viscosity)
    forward, backward = shifts("rad")
    rad_lo = lax.ppermute(rad_top, "rad", forward)
    rad_hi = lax.ppermute(rad_bottom, "rad", backward)
    ax_top, ax_bottom = face_call(velocity, after(viscosity, rad_top))
    az = split_call(after(az_inverse, ax_top))
    rad = half_call(after(side, az[0]), rad_inverse)
    forward, backward = shifts("ax")
    ax_top, ax_bottom, rad_lo, rad_hi, *_ = lax.optimization_barrier(
        (ax_top, ax_bottom, rad_lo, rad_hi, az[0], rad[0])
    )
    ax_lo = lax.ppermute(ax_top, "ax", forward)
    ax_hi = lax.ppermute(ax_bottom, "ax", backward)
    groups = [list(range(0, lines, 2)), list(range(1, lines, 2))]

    def exchange(x):
        return lax.all_to_all(
            x, "rad", split_axis=0, concat_axis=0, tiled=True, axis_index_groups=groups
        )

    def partner(x):
        return lax.ppermute(x, "rad", [(i, i ^ 1) for i in range(lines)])

    common = (inv_dr, inv_rt, velocity, viscosity, rad_lo, rad_hi)
    (first,) = rhs_call(CHUNKS[:1], parts, inv_dx, *common, (), az)
    (second,) = rhs_call(CHUNKS[1:2], parts, after(inv_dx, first), *common, (), az)
    second, ax_lo, ax_hi = lax.optimization_barrier((second, ax_lo, ax_hi))
    own = [exchange(first)]
    other = [partner(after(own[0], ax_lo))]
    own.append(exchange(after(second, own[0])))
    edges = rhs_call(CHUNKS[2:], parts, after(inv_dx, own[0]), *common, (ax_lo, ax_hi), az)
    other.append(partner(after(own[1], edges[0])))
    solved = [radial_call(rad, own[k], other[k], RADIAL_BYTES[k]) for k in range(2)]
    own.append(exchange(after(edges[0], own[1])))
    own.append(exchange(after(edges[1], own[2], solved[0])))
    back = [exchange(after(solved[0], own[3], other[1]))]
    for k in range(2, len(CHUNKS)):
        other.append(partner(after(own[k], other[k - 2])))
        solved.append(radial_call(rad, own[k], other[k], RADIAL_BYTES[k]))
    whole = place_call(CHUNKS[0], back[0], None, velocity.shape)
    for k in range(1, len(CHUNKS)):
        back.append(exchange(after(solved[k], back[-1])))
        whole = place_call(CHUNKS[k], back[k], whole, velocity.shape)
    return whole


def solution(mesh):
    placed = (
        P(None, "ax", "rad", None),
        P("ax", "rad", None),
        P("ax"),
        P("rad"),
        P("rad"),
        P(),
        P(),
    )
    return jax.shard_map(
        local, mesh=mesh, in_specs=placed, out_specs=P(None, "ax", "rad", None), check_vma=False
    )
```

```python
import functools

import jax
import jax.numpy as jnp
from jax import lax
from jax.experimental import pallas as pl
from jax.experimental.pallas import tpu as pltpu
from jax.sharding import PartitionSpec as P

COEF = 0.25
F32 = jnp.float32
BF16 = jnp.bfloat16
INNER = ((2, 3), (4, 5))
OUTER = ((0, 1), (6, 7))
HALF_BYTES = 200 * 1024 * 1024
COLUMNS = 256
VMEM_LIMIT = 56 * 1024 * 1024


def split(x):
    hi = x.astype(BF16)
    return hi, (x - hi.astype(F32)).astype(BF16)


def dot3(a_hi, a_lo, b_hi, b_lo, dims):
    dot = functools.partial(
        lax.dot_general, dimension_numbers=(dims, ((), ())), preferred_element_type=F32
    )
    return dot(a_hi, b_hi) + (dot(a_hi, b_lo) + dot(a_lo, b_hi))


def split_kernel(x_ref, hi_ref, lo_ref):
    hi_ref[...], lo_ref[...] = split(x_ref[...].T)


def split_call(x):
    rows, cols = x.shape
    spec = pl.BlockSpec((256, cols), lambda i: (i, 0))
    return pl.pallas_call(
        split_kernel,
        name=f"split_{rows}",
        grid=(rows // 256,),
        in_specs=[spec],
        out_specs=[pl.BlockSpec((cols, 256), lambda i: (0, i))] * 2,
        out_shape=[jax.ShapeDtypeStruct((cols, rows), BF16)] * 2,
    )(x)


def rhs_kernel(
    groups, edge, inv_dx, inv_dr, inv_rt, velocity, viscosity, rad_lo, rad_hi, *rest
):
    if edge:
        ax_lo, ax_hi, az_hi, az_lo, *outs = rest
    else:
        az_hi, az_lo, *outs = rest
    *outs, vbuf, nbuf, rhs, hi, lo, sems = outs
    planes, rows, nt = viscosity.shape
    width = outs[0].shape[3]
    copies = []

    def bring(source, target):
        copy = pltpu.make_async_copy(source, target, sems.at[len(copies)])
        copy.start()
        copies.append(copy)

    chosen = [p for group in groups for p in group]
    first, last = max(min(chosen) - 2, 0), min(max(chosen) + 3, planes)
    inner, mine = pl.ds(8, rows), pl.ds(first, last - first)
    held = pl.ds(first + 2, last - first)
    for c in range(3):
        bring(velocity.at[c, mine], vbuf.at[c, held, inner])
    bring(viscosity.at[mine], nbuf.at[held, inner])
    if edge:
        for halo, at, thin in ((ax_lo, 0, 1), (ax_hi, planes + 2, planes + 2)):
            for c in range(3):
                bring(halo.at[pl.ds(2 * c, 2)], vbuf.at[c, pl.ds(at, 2), inner])
            bring(halo.at[6], nbuf.at[thin, inner])
    for copy in copies:
        copy.wait()

    def stencil(place, p):
        at = p + 2
        low, high = rad_lo[p], rad_hi[p]
        for c in range(3):
            vbuf[c, at, 0:8, :] = pltpu.roll(low, 6 - 2 * c, 0)
            vbuf[c, at, rows + 8 : rows + 16, :] = pltpu.roll(high, (8 - 2 * c) % 8, 0)
        nbuf[at, 0:8, :] = pltpu.roll(low, 1, 0)
        nbuf[at, rows + 8 : rows + 16, :] = pltpu.roll(high, 2, 0)
        gx = inv_dx[p]

        def strip(i, carry):
            r0 = pl.multiple_of(i * 8, 8)
            mid = pl.ds(pl.multiple_of(r0 + 8, 8), 8)
            wide = pl.ds(r0, 24)
            metrics = (gx, inv_rt[pl.ds(r0, 8), :], inv_dr[pl.ds(r0, 8), :])
            metrics = tuple(
                (g, (0.5 * COEF) * g * g, (COEF / 12.0) * g) for g in metrics
            )
            for l0 in range(0, nt, COLUMNS):
                cols = pl.ds(l0, COLUMNS)
                before, behind = pl.ds((l0 - 128) % nt, 128), pl.ds((l0 + COLUMNS) % nt, 128)

                def turned(ref, *shifts):
                    ext = jnp.concatenate(
                        [ref[mid, before], ref[mid, cols], ref[mid, behind]], axis=1
                    )
                    size = COLUMNS + 256
                    return [
                        pltpu.roll(ext, shift % size, 1)[:, 128 : 128 + COLUMNS]
                        for shift in shifts
                    ]

                nu24 = nbuf[at, wide, cols]
                nu = nu24[8:16]
                nus = (
                    (nbuf[at + 1, mid, cols], nbuf[at - 1, mid, cols]),
                    turned(nbuf.at[at], -1, 1),
                    (nu24[9:17], nu24[7:15]),
                )
                coefs = []
                centre = None
                for d, ((up, down), (_, gg, g12)) in enumerate(zip(nus, metrics)):
                    a_up = gg * (nu + up)
                    a_down = gg * (nu + down)
                    b = g12 * vbuf[d, at, mid, cols]
                    b8 = 8.0 * b
                    total = a_up + a_down
                    centre = total if centre is None else centre + total
                    coefs.append((a_up - b8, a_down + b8, b))
                centre = 1.0 - centre
                for c in range(3):
                    q24 = vbuf[c, at, wide, cols]
                    near = (
                        [vbuf[c, at + k, mid, cols] for k in (1, -1, 2, -2)],
                        turned(vbuf.at[c, at], -1, 1, -2, 2),
                        [q24[8 + k : 16 + k] for k in (1, -1, 2, -2)],
                    )
                    total = centre * q24[8:16]
                    for (up, down, up2, down2), (c_up, c_down, b) in zip(near, coefs):
                        total = total + (c_up * up + c_down * down + b * (up2 - down2))
                    rhs[place, c, pl.ds(r0, 8), cols] = total
            return carry

        lax.fori_loop(0, rows // 8, strip, 0)

    for group, out in zip(groups, outs):
        size = len(group)

        low = sum(p < group[0] + len(group) for p in group)
        jump = group[-1] - group[0] - size + 1

        def plane(j, carry):
            stencil(j, group[0] + j + jnp.where(j >= low, jump, 0))
            return carry

        lax.fori_loop(0, size, plane, 0)
        lines = size * rows
        hi[0 : 3 * lines, :], lo[0 : 3 * lines, :] = split(rhs[0:size].reshape(3 * lines, nt))
        for d in range(nt // width):
            cols = pl.ds(d * width, width)
            solved = dot3(
                hi[0 : 3 * lines, :], lo[0 : 3 * lines, :], az_hi[:, cols], az_lo[:, cols],
                ((1,), (0,)),
            )
            out[d] = solved.reshape(3 * size, rows, width)


def rhs_call(groups, parts, inv_dx, inv_dr, inv_rt, velocity, viscosity, rad_lo, rad_hi, ax, az):
    rows, nt = velocity.shape[2], velocity.shape[3]
    anywhere = pl.BlockSpec(memory_space=pl.ANY)
    vmem = pl.BlockSpec(memory_space=pltpu.VMEM)
    most = max(len(group) for group in groups)
    return pl.pallas_call(
        functools.partial(rhs_kernel, groups, bool(ax)),
        name=f"rhs_{groups[0][0]}",
        in_specs=[pl.BlockSpec(memory_space=pltpu.SMEM), vmem, vmem, anywhere, anywhere, vmem, vmem]
        + [anywhere] * len(ax)
        + [vmem, vmem],
        out_specs=[vmem] * len(groups),
        out_shape=[
            jax.ShapeDtypeStruct((parts, 3 * len(group), rows, nt // parts), F32)
            for group in groups
        ],
        scratch_shapes=[
            pltpu.VMEM((3, 12, rows + 16, nt), F32),
            pltpu.VMEM((12, rows + 16, nt), F32),
            pltpu.VMEM((most, 3, rows, nt), F32),
            pltpu.VMEM((3 * most * rows, nt), BF16),
            pltpu.VMEM((3 * most * rows, nt), BF16),
            pltpu.SemaphoreType.DMA((12,)),
        ],
        compiler_params=pltpu.CompilerParams(vmem_limit_bytes=VMEM_LIMIT),
        cost_estimate=pl.CostEstimate(flops=1024, bytes_accessed=1024, transcendentals=0),
    )(inv_dx, inv_dr[:, None], inv_rt[:, None], velocity, viscosity, rad_lo, rad_hi, *ax, *az)


def half_kernel(side_ref, x_ref, hi_ref, lo_ref, hi_far_ref, lo_far_ref):
    rows = x_ref.shape[0] // 8
    side = side_ref[0]
    for part in range(4):
        at = slice(part * rows, (part + 1) * rows)
        for one, hi, lo in ((side, hi_ref, lo_ref), (1 - side, hi_far_ref, lo_far_ref)):
            x = x_ref[pl.ds(pl.multiple_of(part * 2 * rows + one * rows, rows), rows), :]
            swapped = jnp.concatenate(
                [
                    pltpu.roll(x[:, low : low + 2 * rows], rows, 1)
                    for low in range(0, x.shape[1], 2 * rows)
                ],
                axis=1,
            )
            hi[at, :], lo[at, :] = split(jnp.where(side == 0, x, swapped))


def half_call(side, x):
    rows, cols = x.shape
    vmem = pl.BlockSpec(memory_space=pltpu.VMEM)
    return pl.pallas_call(
        half_kernel,
        name="half",
        in_specs=[pl.BlockSpec(memory_space=pltpu.SMEM), vmem],
        out_specs=[vmem] * 4,
        out_shape=[jax.ShapeDtypeStruct((rows // 2, cols), BF16)] * 4,
    )(side, x)


def radial_kernel(r_hi, r_lo, own_ref, *rest):
    *others, out_ref = rest
    parts, slabs, rows, width = own_ref.shape
    theirs = [(ref, part) for ref in others for part in range(ref.shape[0])]
    x = jnp.concatenate(
        [
            jnp.concatenate(
                [
                    ref[at, s]
                    for part in range(parts)
                    for ref, at in ((own_ref, part), theirs[part])
                ],
                axis=0,
            )
            for s in range(slabs)
        ],
        axis=1,
    )
    hi, lo = split(x)
    y = dot3(r_hi[...], r_lo[...], hi, lo, ((1,), (0,)))
    for s in range(slabs):
        out_ref[:, s] = y[:, s * width : (s + 1) * width].reshape(parts, rows, width)


def radial_call(rad, own, others):
    parts, slabs, rows, width = own.shape

    def block(x):
        return pl.BlockSpec((x.shape[0], 3, rows, width), lambda i: (0, i, 0, 0))

    full = pl.BlockSpec(rad[0].shape, lambda i: (0, 0))
    return pl.pallas_call(
        radial_kernel,
        name="radial",
        grid=(slabs // 3,),
        in_specs=[full, full, block(own)] + [block(x) for x in others],
        out_specs=block(own),
        out_shape=jax.ShapeDtypeStruct(own.shape, F32),
        compiler_params=pltpu.CompilerParams(vmem_limit_bytes=VMEM_LIMIT),
        cost_estimate=pl.CostEstimate(flops=1024, bytes_accessed=1024, transcendentals=0),
    )(*rad, own, *others)


def both_kernel(side_ref, r_hi, r_lo, f_hi, f_lo, own_ref, other_ref, out_ref):
    parts, slabs, rows, width = other_ref.shape
    mine = pl.ds(pl.multiple_of(side_ref[0] * width, width), width)
    x = jnp.concatenate(
        [
            jnp.concatenate(
                [
                    piece
                    for part in range(parts)
                    for piece in (own_ref[part, s, :, mine], other_ref[part, s])
                ],
                axis=0,
            )
            for s in range(slabs)
        ],
        axis=1,
    )
    hi, lo = split(x)
    for way, (a_hi, a_lo) in enumerate(((r_hi, r_lo), (f_hi, f_lo))):
        y = dot3(a_hi[...], a_lo[...], hi, lo, ((1,), (0,)))
        for s in range(slabs):
            out_ref[:, way, s] = y[:, s * width : (s + 1) * width].reshape(parts, rows, width)


def both_call(side, rad, own, other):
    parts, slabs, rows, width = other.shape
    full = pl.BlockSpec(rad[0].shape, lambda i: (0, 0))
    return pl.pallas_call(
        both_kernel,
        name="radial_both",
        grid=(slabs // 3,),
        in_specs=[pl.BlockSpec(memory_space=pltpu.SMEM)]
        + [full] * 4
        + [
            pl.BlockSpec((parts, 3, rows, 2 * width), lambda i: (0, i, 0, 0)),
            pl.BlockSpec((parts, 3, rows, width), lambda i: (0, i, 0, 0)),
        ],
        out_specs=pl.BlockSpec((parts, 2, 3, rows, width), lambda i: (0, 0, i, 0, 0)),
        out_shape=jax.ShapeDtypeStruct((parts, 2, slabs, rows, width), F32),
        compiler_params=pltpu.CompilerParams(vmem_limit_bytes=VMEM_LIMIT),
        cost_estimate=pl.CostEstimate(flops=1024, bytes_accessed=1024, transcendentals=0),
    )(side, *rad, own, other)


def weave_kernel(side_ref, near_ref, far_ref, _, out_ref):
    parts, _, _, _, width = near_ref.shape
    side = side_ref[0]
    for d in range(parts):
        for c in range(3):
            for at, value in ((side, near_ref[d, 0, c]), (1 - side, far_ref[d, c])):
                cols = pl.ds(pl.multiple_of((2 * d + at) * width, width), width)
                out_ref[c, 0, :, cols] = value


def weave_call(side, planes, near, far, whole):
    parts, _, rows, width = far.shape
    first = planes[0]
    return pl.pallas_call(
        weave_kernel,
        name="weave",
        grid=(len(planes),),
        in_specs=[
            pl.BlockSpec(memory_space=pltpu.SMEM),
            pl.BlockSpec((parts, 1, 3, rows, width), lambda j: (0, 0, j, 0, 0)),
            pl.BlockSpec((parts, 3, rows, width), lambda j: (0, j, 0, 0)),
            pl.BlockSpec(memory_space=pl.ANY),
        ],
        out_specs=pl.BlockSpec((3, 1, rows, 2 * parts * width), lambda j: (0, first + j, 0, 0)),
        out_shape=jax.ShapeDtypeStruct(whole.shape, F32),
        input_output_aliases={3: 0},
        cost_estimate=pl.CostEstimate(flops=0, bytes_accessed=16 * far.size, transcendentals=0),
    )(side, near, far, whole)


def place_kernel(x_ref, *rest):
    out_ref = rest[-1]
    parts, width = x_ref.shape[0], x_ref.shape[3]
    for d in range(parts):
        for c in range(3):
            out_ref[c, 0, :, d * width : (d + 1) * width] = x_ref[d, c]


def place_call(planes, x, whole, shape):
    parts, _, rows, width = x.shape
    first = planes[0]
    aliased = () if whole is None else (whole,)
    return pl.pallas_call(
        place_kernel,
        name="place",
        grid=(len(planes),),
        in_specs=[pl.BlockSpec((parts, 3, rows, width), lambda j: (0, j, 0, 0))]
        + [pl.BlockSpec(memory_space=pl.ANY)] * len(aliased),
        out_specs=pl.BlockSpec((3, 1, rows, parts * width), lambda j: (0, first + j, 0, 0)),
        out_shape=jax.ShapeDtypeStruct(shape, F32),
        input_output_aliases={1: 0} if aliased else {},
        cost_estimate=pl.CostEstimate(flops=0, bytes_accessed=8 * x.size, transcendentals=0),
    )(x, *aliased)


def line_kernel(velocity, viscosity, top, bottom, edges, sems):
    planes, rows = viscosity.shape[0], viscosity.shape[1]
    copies = []
    for side, at in enumerate((rows - 8, 0)):
        for f in range(4):
            source = velocity.at[f, :, pl.ds(at, 8)] if f < 3 else viscosity.at[:, pl.ds(at, 8)]
            copies.append(
                pltpu.make_async_copy(source, edges.at[side, f], sems.at[len(copies)])
            )
    for copy in copies:
        copy.start()
    for copy in copies:
        copy.wait()
    row = lax.broadcasted_iota(jnp.int32, edges.shape[3:], 0)
    for p in range(planes):
        for side, out, turns in ((0, top, (2, 4, 6, 7)), (1, bottom, (0, 2, 4, 6))):
            strips = [
                pltpu.roll(edges[side, f, p], turn, 0) if turn else edges[side, f, p]
                for f, turn in enumerate(turns)
            ]
            out[p] = jnp.where(
                row < 4,
                jnp.where(row < 2, strips[0], strips[1]),
                jnp.where(row < 6, strips[2], strips[3]),
            )


def line_call(velocity, viscosity):
    planes, _, nt = viscosity.shape
    anywhere = pl.BlockSpec(memory_space=pl.ANY)
    vmem = pl.BlockSpec(memory_space=pltpu.VMEM)
    return pl.pallas_call(
        line_kernel,
        name="lines",
        in_specs=[anywhere, anywhere],
        out_specs=[vmem, vmem],
        out_shape=[jax.ShapeDtypeStruct((planes, 8, nt), F32)] * 2,
        scratch_shapes=[pltpu.VMEM((2, 4, planes, 8, nt), F32), pltpu.SemaphoreType.DMA((8,))],
        compiler_params=pltpu.CompilerParams(vmem_limit_bytes=VMEM_LIMIT),
    )(velocity, viscosity)


def face_kernel(velocity, viscosity, top, bottom, sems):
    planes = viscosity.shape[0]
    copies = []
    for out, at, thin in ((top, planes - 2, planes - 1), (bottom, 0, 0)):
        for f in range(4):
            source = velocity.at[f, pl.ds(at, 2)] if f < 3 else viscosity.at[pl.ds(thin, 1)]
            target = out.at[pl.ds(2 * f, 2 if f < 3 else 1)]
            copies.append(pltpu.make_async_copy(source, target, sems.at[len(copies)]))
    for copy in copies:
        copy.start()
    for copy in copies:
        copy.wait()


def face_call(velocity, viscosity):
    _, rows, nt = viscosity.shape
    anywhere = pl.BlockSpec(memory_space=pl.ANY)
    vmem = pl.BlockSpec(memory_space=pltpu.VMEM)
    return pl.pallas_call(
        face_kernel,
        name="faces",
        in_specs=[anywhere, anywhere],
        out_specs=[vmem, vmem],
        out_shape=[jax.ShapeDtypeStruct((7, rows, nt), F32)] * 2,
        scratch_shapes=[pltpu.SemaphoreType.DMA((8,))],
        compiler_params=pltpu.CompilerParams(vmem_limit_bytes=VMEM_LIMIT),
    )(velocity, viscosity)


def after(x, *events):
    return lax.optimization_barrier((x, *events))[0]


def local(velocity, viscosity, inv_dx, inv_dr, inv_rt, az_inverse, rad_inverse):
    planes = velocity.shape[1]
    lines = lax.axis_size("rad")
    parts = lines // 2
    side = (lax.axis_index("rad") % 2).astype(jnp.int32).reshape(1)

    def shifts(axis):
        count = lax.axis_size(axis)
        forward = [(i, i + 1) for i in range(count - 1)]
        return forward, [(b, a) for a, b in forward]

    rad_top, rad_bottom = line_call(velocity, viscosity)
    forward, backward = shifts("rad")
    rad_lo = lax.ppermute(rad_top, "rad", forward)
    rad_hi = lax.ppermute(rad_bottom, "rad", backward)
    ax_top, ax_bottom = face_call(velocity, after(viscosity, rad_top))
    az = split_call(after(az_inverse, ax_top))
    forward, backward = shifts("ax")
    ax_top, ax_bottom, rad_lo, rad_hi, *_ = lax.optimization_barrier(
        (ax_top, ax_bottom, rad_lo, rad_hi, az[0])
    )
    ax_lo = lax.ppermute(ax_top, "ax", forward)
    ax_hi = lax.ppermute(ax_bottom, "ax", backward)
    groups = [list(range(0, lines, 2)), list(range(1, lines, 2))]

    def exchange(x):
        return lax.all_to_all(
            x, "rad", split_axis=0, concat_axis=0, tiled=True, axis_index_groups=groups
        )

    def partner(x):
        return lax.ppermute(x, "rad", [(i, i ^ 1) for i in range(lines)])

    common = (inv_dr, inv_rt, velocity, viscosity, rad_lo, rad_hi)
    (first,) = rhs_call(INNER[:1], parts, inv_dx, *common, (), az)
    rad = half_call(after(side, first), rad_inverse)
    (second,) = rhs_call(INNER[1:], parts, after(inv_dx, first, rad[0]), *common, (), az)
    second, ax_lo, ax_hi = lax.optimization_barrier((second, ax_lo, ax_hi))
    own = [exchange(first)]
    other = [(partner(after(own[0], ax_lo)),)]
    own.append(exchange(after(second, own[0])))
    edges = rhs_call(OUTER, parts, after(inv_dx, own[0]), *common, (ax_lo, ax_hi), az)
    own.append(exchange(after(edges[0], own[1])))
    other.append((partner(after(own[1], edges[0])),))
    solved = [radial_call(rad[:2], own[k], other[k]) for k in range(2)]
    own.append(exchange(after(edges[1], own[2], solved[0])))
    width = own[2].shape[3] // 2
    sent = lax.dynamic_slice_in_dim(own[2], (1 - side[0]) * width, width, axis=3)
    sent = partner(after(sent, other[0][0]))
    other.append((partner(after(own[3], other[1][0])),))
    backs = [exchange(after(solved[0], own[3], other[1][0]))]
    backs.append(exchange(after(solved[1], backs[0], sent)))
    near = exchange(after(both_call(side, rad, own[2], sent), backs[1]))
    far = partner(near[:, 1])
    backs.append(exchange(after(radial_call(rad[:2], own[3], other[2]), near)))
    whole = None
    for planes_of, back in zip((*INNER, OUTER[1]), backs):
        whole = place_call(planes_of, back, whole, velocity.shape)
    whole = weave_call(side, OUTER[0], near, far, whole)
    return whole


def solution(mesh):
    placed = (
        P(None, "ax", "rad", None),
        P("ax", "rad", None),
        P("ax"),
        P("rad"),
        P("rad"),
        P(),
        P(),
    )
    return jax.shard_map(
        local, mesh=mesh, in_specs=placed, out_specs=P(None, "ax", "rad", None), check_vma=False
    )
```

```python
import functools

import jax
import jax.numpy as jnp
from jax import lax
from jax.experimental import pallas as pl
from jax.experimental.pallas import tpu as pltpu
from jax.sharding import PartitionSpec as P

COEF = 0.25
F32 = jnp.float32
BF16 = jnp.bfloat16
INNER = ((2, 3), (4, 5))
OUTER = ((0, 1), (6, 7))
HALF_BYTES = 200 * 1024 * 1024
COLUMNS = 512
VMEM_LIMIT = 56 * 1024 * 1024


def split(x):
    hi = x.astype(BF16)
    return hi, (x - hi.astype(F32)).astype(BF16)


def dot3(a_hi, a_lo, b_hi, b_lo, dims):
    dot = functools.partial(
        lax.dot_general, dimension_numbers=(dims, ((), ())), preferred_element_type=F32
    )
    return dot(a_hi, b_hi) + (dot(a_hi, b_lo) + dot(a_lo, b_hi))


def split_kernel(x_ref, hi_ref, lo_ref):
    hi_ref[...], lo_ref[...] = split(x_ref[...].T)


def split_call(x):
    rows, cols = x.shape
    spec = pl.BlockSpec((256, cols), lambda i: (i, 0))
    return pl.pallas_call(
        split_kernel,
        name=f"split_{rows}",
        grid=(rows // 256,),
        in_specs=[spec],
        out_specs=[pl.BlockSpec((cols, 256), lambda i: (0, i))] * 2,
        out_shape=[jax.ShapeDtypeStruct((cols, rows), BF16)] * 2,
    )(x)


def rhs_kernel(
    groups, edge, inv_dx, inv_dr, inv_rt, velocity, viscosity, rad_lo, rad_hi, *rest
):
    if edge:
        ax_lo, ax_hi, az_hi, az_lo, *outs = rest
    else:
        az_hi, az_lo, *outs = rest
    *outs, vbuf, nbuf, rhs, hi, lo, sems = outs
    planes, rows, nt = viscosity.shape
    width = outs[0].shape[3]
    copies = []

    def bring(source, target):
        copy = pltpu.make_async_copy(source, target, sems.at[len(copies)])
        copy.start()
        copies.append(copy)

    chosen = [p for group in groups for p in group]
    first, last = max(min(chosen) - 2, 0), min(max(chosen) + 3, planes)
    inner, mine = pl.ds(8, rows), pl.ds(first, last - first)
    held = pl.ds(first + 2, last - first)
    for c in range(3):
        bring(velocity.at[c, mine], vbuf.at[c, held, inner])
    bring(viscosity.at[mine], nbuf.at[held, inner])
    if edge:
        for halo, at, thin in ((ax_lo, 0, 1), (ax_hi, planes + 2, planes + 2)):
            for c in range(3):
                bring(halo.at[pl.ds(2 * c, 2)], vbuf.at[c, pl.ds(at, 2), inner])
            bring(halo.at[6], nbuf.at[thin, inner])
    for copy in copies:
        copy.wait()

    def stencil(place, p):
        at = p + 2
        low, high = rad_lo[p], rad_hi[p]
        for c in range(3):
            vbuf[c, at, 0:8, :] = pltpu.roll(low, 6 - 2 * c, 0)
            vbuf[c, at, rows + 8 : rows + 16, :] = pltpu.roll(high, (8 - 2 * c) % 8, 0)
        nbuf[at, 0:8, :] = pltpu.roll(low, 1, 0)
        nbuf[at, rows + 8 : rows + 16, :] = pltpu.roll(high, 2, 0)
        gx = inv_dx[p]

        def strip(i, carry):
            r0 = pl.multiple_of(i * 8, 8)
            mid = pl.ds(pl.multiple_of(r0 + 8, 8), 8)
            wide = pl.ds(r0, 24)
            metrics = (gx, inv_rt[pl.ds(r0, 8), :], inv_dr[pl.ds(r0, 8), :])
            metrics = tuple(
                (g, (0.5 * COEF) * g * g, (COEF / 12.0) * g) for g in metrics
            )
            for l0 in range(0, nt, COLUMNS):
                cols = pl.ds(l0, COLUMNS)
                before, behind = pl.ds((l0 - 128) % nt, 128), pl.ds((l0 + COLUMNS) % nt, 128)

                def turned(ref, *shifts):
                    ext = jnp.concatenate(
                        [ref[mid, before], ref[mid, cols], ref[mid, behind]], axis=1
                    )
                    size = COLUMNS + 256
                    return [
                        pltpu.roll(ext, shift % size, 1)[:, 128 : 128 + COLUMNS]
                        for shift in shifts
                    ]

                nu24 = nbuf[at, wide, cols]
                nu = nu24[8:16]
                nus = (
                    (nbuf[at + 1, mid, cols], nbuf[at - 1, mid, cols]),
                    turned(nbuf.at[at], -1, 1),
                    (nu24[9:17], nu24[7:15]),
                )
                coefs = []
                centre = None
                for d, ((up, down), (_, gg, g12)) in enumerate(zip(nus, metrics)):
                    a_up = gg * (nu + up)
                    a_down = gg * (nu + down)
                    b = g12 * vbuf[d, at, mid, cols]
                    b8 = 8.0 * b
                    total = a_up + a_down
                    centre = total if centre is None else centre + total
                    coefs.append((a_up - b8, a_down + b8, b))
                centre = 1.0 - centre
                for c in range(3):
                    q24 = vbuf[c, at, wide, cols]
                    near = (
                        [vbuf[c, at + k, mid, cols] for k in (1, -1, 2, -2)],
                        turned(vbuf.at[c, at], -1, 1, -2, 2),
                        [q24[8 + k : 16 + k] for k in (1, -1, 2, -2)],
                    )
                    total = centre * q24[8:16]
                    for (up, down, up2, down2), (c_up, c_down, b) in zip(near, coefs):
                        total = total + (c_up * up + c_down * down + b * (up2 - down2))
                    rhs[place, c, pl.ds(r0, 8), cols] = total
            return carry

        lax.fori_loop(0, rows // 8, strip, 0)

    for group, out in zip(groups, outs):
        size = len(group)

        low = sum(p < group[0] + len(group) for p in group)
        jump = group[-1] - group[0] - size + 1

        def plane(j, carry):
            stencil(j, group[0] + j + jnp.where(j >= low, jump, 0))
            return carry

        lax.fori_loop(0, size, plane, 0)
        lines = size * rows
        hi[0 : 3 * lines, :], lo[0 : 3 * lines, :] = split(rhs[0:size].reshape(3 * lines, nt))
        for d in range(nt // width):
            cols = pl.ds(d * width, width)
            solved = dot3(
                hi[0 : 3 * lines, :], lo[0 : 3 * lines, :], az_hi[:, cols], az_lo[:, cols],
                ((1,), (0,)),
            )
            out[d] = solved.reshape(3 * size, rows, width)


def rhs_call(groups, parts, inv_dx, inv_dr, inv_rt, velocity, viscosity, rad_lo, rad_hi, ax, az):
    rows, nt = velocity.shape[2], velocity.shape[3]
    anywhere = pl.BlockSpec(memory_space=pl.ANY)
    vmem = pl.BlockSpec(memory_space=pltpu.VMEM)
    most = max(len(group) for group in groups)
    return pl.pallas_call(
        functools.partial(rhs_kernel, groups, bool(ax)),
        name=f"rhs_{groups[0][0]}",
        in_specs=[pl.BlockSpec(memory_space=pltpu.SMEM), vmem, vmem, anywhere, anywhere, vmem, vmem]
        + [anywhere] * len(ax)
        + [vmem, vmem],
        out_specs=[vmem] * len(groups),
        out_shape=[
            jax.ShapeDtypeStruct((parts, 3 * len(group), rows, nt // parts), F32)
            for group in groups
        ],
        scratch_shapes=[
            pltpu.VMEM((3, 12, rows + 16, nt), F32),
            pltpu.VMEM((12, rows + 16, nt), F32),
            pltpu.VMEM((most, 3, rows, nt), F32),
            pltpu.VMEM((3 * most * rows, nt), BF16),
            pltpu.VMEM((3 * most * rows, nt), BF16),
            pltpu.SemaphoreType.DMA((12,)),
        ],
        compiler_params=pltpu.CompilerParams(vmem_limit_bytes=VMEM_LIMIT),
        cost_estimate=pl.CostEstimate(flops=1024, bytes_accessed=1024, transcendentals=0),
    )(inv_dx, inv_dr[:, None], inv_rt[:, None], velocity, viscosity, rad_lo, rad_hi, *ax, *az)


def half_kernel(side_ref, x_ref, hi_ref, lo_ref, hi_far_ref, lo_far_ref):
    rows = x_ref.shape[0] // 8
    side = side_ref[0]
    for part in range(4):
        at = slice(part * rows, (part + 1) * rows)
        for one, hi, lo in ((side, hi_ref, lo_ref), (1 - side, hi_far_ref, lo_far_ref)):
            x = x_ref[pl.ds(pl.multiple_of(part * 2 * rows + one * rows, rows), rows), :]
            swapped = jnp.concatenate(
                [
                    pltpu.roll(x[:, low : low + 2 * rows], rows, 1)
                    for low in range(0, x.shape[1], 2 * rows)
                ],
                axis=1,
            )
            hi[at, :], lo[at, :] = split(jnp.where(side == 0, x, swapped))


def half_call(side, x):
    rows, cols = x.shape
    vmem = pl.BlockSpec(memory_space=pltpu.VMEM)
    return pl.pallas_call(
        half_kernel,
        name="half",
        in_specs=[pl.BlockSpec(memory_space=pltpu.SMEM), vmem],
        out_specs=[vmem] * 4,
        out_shape=[jax.ShapeDtypeStruct((rows // 2, cols), BF16)] * 4,
    )(side, x)


def radial_kernel(r_hi, r_lo, own_ref, *rest):
    *others, out_ref = rest
    parts, slabs, rows, width = own_ref.shape
    theirs = [(ref, part) for ref in others for part in range(ref.shape[0])]
    x = jnp.concatenate(
        [
            jnp.concatenate(
                [
                    ref[at, s]
                    for part in range(parts)
                    for ref, at in ((own_ref, part), theirs[part])
                ],
                axis=0,
            )
            for s in range(slabs)
        ],
        axis=1,
    )
    hi, lo = split(x)
    y = dot3(r_hi[...], r_lo[...], hi, lo, ((1,), (0,)))
    for s in range(slabs):
        out_ref[:, s] = y[:, s * width : (s + 1) * width].reshape(parts, rows, width)


def radial_call(rad, own, others):
    parts, slabs, rows, width = own.shape

    def block(x):
        return pl.BlockSpec((x.shape[0], 3, rows, width), lambda i: (0, i, 0, 0))

    full = pl.BlockSpec(rad[0].shape, lambda i: (0, 0))
    return pl.pallas_call(
        radial_kernel,
        name="radial",
        grid=(slabs // 3,),
        in_specs=[full, full, block(own)] + [block(x) for x in others],
        out_specs=block(own),
        out_shape=jax.ShapeDtypeStruct(own.shape, F32),
        compiler_params=pltpu.CompilerParams(vmem_limit_bytes=VMEM_LIMIT),
        cost_estimate=pl.CostEstimate(flops=1024, bytes_accessed=1024, transcendentals=0),
    )(*rad, own, *others)


def both_kernel(side_ref, r_hi, r_lo, f_hi, f_lo, own_ref, other_ref, out_ref):
    parts, slabs, rows, width = other_ref.shape
    mine = pl.ds(pl.multiple_of(side_ref[0] * width, width), width)
    x = jnp.concatenate(
        [
            jnp.concatenate(
                [
                    piece
                    for part in range(parts)
                    for piece in (own_ref[part, s, :, mine], other_ref[part, s])
                ],
                axis=0,
            )
            for s in range(slabs)
        ],
        axis=1,
    )
    hi, lo = split(x)
    for way, (a_hi, a_lo) in enumerate(((r_hi, r_lo), (f_hi, f_lo))):
        y = dot3(a_hi[...], a_lo[...], hi, lo, ((1,), (0,)))
        for s in range(slabs):
            out_ref[:, way, s] = y[:, s * width : (s + 1) * width].reshape(parts, rows, width)


def both_call(side, rad, own, other):
    parts, slabs, rows, width = other.shape
    full = pl.BlockSpec(rad[0].shape, lambda i: (0, 0))
    return pl.pallas_call(
        both_kernel,
        name="radial_both",
        grid=(slabs // 3,),
        in_specs=[pl.BlockSpec(memory_space=pltpu.SMEM)]
        + [full] * 4
        + [
            pl.BlockSpec((parts, 3, rows, 2 * width), lambda i: (0, i, 0, 0)),
            pl.BlockSpec((parts, 3, rows, width), lambda i: (0, i, 0, 0)),
        ],
        out_specs=pl.BlockSpec((parts, 2, 3, rows, width), lambda i: (0, 0, i, 0, 0)),
        out_shape=jax.ShapeDtypeStruct((parts, 2, slabs, rows, width), F32),
        compiler_params=pltpu.CompilerParams(vmem_limit_bytes=VMEM_LIMIT),
        cost_estimate=pl.CostEstimate(flops=1024, bytes_accessed=1024, transcendentals=0),
    )(side, *rad, own, other)


def weave_kernel(side_ref, near_ref, far_ref, _, out_ref):
    parts, _, _, _, width = near_ref.shape
    side = side_ref[0]
    for d in range(parts):
        for c in range(3):
            for at, value in ((side, near_ref[d, 0, c]), (1 - side, far_ref[d, c])):
                cols = pl.ds(pl.multiple_of((2 * d + at) * width, width), width)
                out_ref[c, 0, :, cols] = value


def weave_call(side, planes, near, far, whole):
    parts, _, rows, width = far.shape
    first = planes[0]
    return pl.pallas_call(
        weave_kernel,
        name="weave",
        grid=(len(planes),),
        in_specs=[
            pl.BlockSpec(memory_space=pltpu.SMEM),
            pl.BlockSpec((parts, 1, 3, rows, width), lambda j: (0, 0, j, 0, 0)),
            pl.BlockSpec((parts, 3, rows, width), lambda j: (0, j, 0, 0)),
            pl.BlockSpec(memory_space=pl.ANY),
        ],
        out_specs=pl.BlockSpec((3, 1, rows, 2 * parts * width), lambda j: (0, first + j, 0, 0)),
        out_shape=jax.ShapeDtypeStruct(whole.shape, F32),
        input_output_aliases={3: 0},
        cost_estimate=pl.CostEstimate(flops=0, bytes_accessed=16 * far.size, transcendentals=0),
    )(side, near, far, whole)


def place_kernel(x_ref, *rest):
    out_ref = rest[-1]
    parts, width = x_ref.shape[0], x_ref.shape[3]
    for d in range(parts):
        for c in range(3):
            out_ref[c, 0, :, d * width : (d + 1) * width] = x_ref[d, c]


def place_call(planes, x, whole, shape):
    parts, _, rows, width = x.shape
    first = planes[0]
    aliased = () if whole is None else (whole,)
    return pl.pallas_call(
        place_kernel,
        name="place",
        grid=(len(planes),),
        in_specs=[pl.BlockSpec((parts, 3, rows, width), lambda j: (0, j, 0, 0))]
        + [pl.BlockSpec(memory_space=pl.ANY)] * len(aliased),
        out_specs=pl.BlockSpec((3, 1, rows, parts * width), lambda j: (0, first + j, 0, 0)),
        out_shape=jax.ShapeDtypeStruct(shape, F32),
        input_output_aliases={1: 0} if aliased else {},
        cost_estimate=pl.CostEstimate(flops=0, bytes_accessed=8 * x.size, transcendentals=0),
    )(x, *aliased)


def line_kernel(velocity, viscosity, top, bottom, edges, sems):
    planes, rows = viscosity.shape[0], viscosity.shape[1]
    copies = []
    for side, at in enumerate((rows - 8, 0)):
        for f in range(4):
            source = velocity.at[f, :, pl.ds(at, 8)] if f < 3 else viscosity.at[:, pl.ds(at, 8)]
            copies.append(
                pltpu.make_async_copy(source, edges.at[side, f], sems.at[len(copies)])
            )
    for copy in copies:
        copy.start()
    for copy in copies:
        copy.wait()
    row = lax.broadcasted_iota(jnp.int32, edges.shape[3:], 0)
    for p in range(planes):
        for side, out, turns in ((0, top, (2, 4, 6, 7)), (1, bottom, (0, 2, 4, 6))):
            strips = [
                pltpu.roll(edges[side, f, p], turn, 0) if turn else edges[side, f, p]
                for f, turn in enumerate(turns)
            ]
            out[p] = jnp.where(
                row < 4,
                jnp.where(row < 2, strips[0], strips[1]),
                jnp.where(row < 6, strips[2], strips[3]),
            )


def line_call(velocity, viscosity):
    planes, _, nt = viscosity.shape
    anywhere = pl.BlockSpec(memory_space=pl.ANY)
    vmem = pl.BlockSpec(memory_space=pltpu.VMEM)
    return pl.pallas_call(
        line_kernel,
        name="lines",
        in_specs=[anywhere, anywhere],
        out_specs=[vmem, vmem],
        out_shape=[jax.ShapeDtypeStruct((planes, 8, nt), F32)] * 2,
        scratch_shapes=[pltpu.VMEM((2, 4, planes, 8, nt), F32), pltpu.SemaphoreType.DMA((8,))],
        compiler_params=pltpu.CompilerParams(vmem_limit_bytes=VMEM_LIMIT),
    )(velocity, viscosity)


def face_kernel(velocity, viscosity, top, bottom, sems):
    planes = viscosity.shape[0]
    copies = []
    for out, at, thin in ((top, planes - 2, planes - 1), (bottom, 0, 0)):
        for f in range(4):
            source = velocity.at[f, pl.ds(at, 2)] if f < 3 else viscosity.at[pl.ds(thin, 1)]
            target = out.at[pl.ds(2 * f, 2 if f < 3 else 1)]
            copies.append(pltpu.make_async_copy(source, target, sems.at[len(copies)]))
    for copy in copies:
        copy.start()
    for copy in copies:
        copy.wait()


def face_call(velocity, viscosity):
    _, rows, nt = viscosity.shape
    anywhere = pl.BlockSpec(memory_space=pl.ANY)
    vmem = pl.BlockSpec(memory_space=pltpu.VMEM)
    return pl.pallas_call(
        face_kernel,
        name="faces",
        in_specs=[anywhere, anywhere],
        out_specs=[vmem, vmem],
        out_shape=[jax.ShapeDtypeStruct((7, rows, nt), F32)] * 2,
        scratch_shapes=[pltpu.SemaphoreType.DMA((8,))],
        compiler_params=pltpu.CompilerParams(vmem_limit_bytes=VMEM_LIMIT),
    )(velocity, viscosity)


def after(x, *events):
    return lax.optimization_barrier((x, *events))[0]


def local(velocity, viscosity, inv_dx, inv_dr, inv_rt, az_inverse, rad_inverse):
    planes = velocity.shape[1]
    lines = lax.axis_size("rad")
    parts = lines // 2
    side = (lax.axis_index("rad") % 2).astype(jnp.int32).reshape(1)

    def shifts(axis):
        count = lax.axis_size(axis)
        forward = [(i, i + 1) for i in range(count - 1)]
        return forward, [(b, a) for a, b in forward]

    rad_top, rad_bottom = line_call(velocity, viscosity)
    forward, backward = shifts("rad")
    rad_lo = lax.ppermute(rad_top, "rad", forward)
    rad_hi = lax.ppermute(rad_bottom, "rad", backward)
    ax_top, ax_bottom = face_call(velocity, after(viscosity, rad_top))
    az = split_call(after(az_inverse, ax_top))
    forward, backward = shifts("ax")
    ax_top, ax_bottom, rad_lo, rad_hi = lax.optimization_barrier(
        (ax_top, ax_bottom, rad_lo, rad_hi)
    )
    ax_lo = lax.ppermute(ax_top, "ax", forward)
    ax_hi = lax.ppermute(ax_bottom, "ax", backward)
    groups = [list(range(0, lines, 2)), list(range(1, lines, 2))]

    def exchange(x):
        return lax.all_to_all(
            x, "rad", split_axis=0, concat_axis=0, tiled=True, axis_index_groups=groups
        )

    def partner(x):
        return lax.ppermute(x, "rad", [(i, i ^ 1) for i in range(lines)])

    common = (inv_dr, inv_rt, velocity, viscosity, rad_lo, rad_hi)
    (first,) = rhs_call(INNER[:1], parts, inv_dx, *common, (), az)
    rad = half_call(after(side, first), rad_inverse)
    (second,) = rhs_call(INNER[1:], parts, after(inv_dx, first, rad[0]), *common, (), az)
    second, ax_lo, ax_hi = lax.optimization_barrier((second, ax_lo, ax_hi))
    own = [exchange(first)]
    other = [(partner(after(own[0], ax_lo)),)]
    own.append(exchange(after(second, own[0])))
    edges = rhs_call(OUTER, parts, after(inv_dx, own[0]), *common, (ax_lo, ax_hi), az)
    own.append(exchange(after(edges[0], own[1])))
    other.append((partner(after(own[1], edges[0])),))
    solved = [radial_call(rad[:2], own[k], other[k]) for k in range(2)]
    own.append(exchange(after(edges[1], own[2], solved[0])))
    width = own[2].shape[3] // 2
    sent = lax.dynamic_slice_in_dim(own[2], (1 - side[0]) * width, width, axis=3)
    sent = partner(after(sent, other[0][0]))
    other.append((partner(after(own[3], other[1][0])),))
    backs = [exchange(after(solved[0], own[3], other[1][0]))]
    backs.append(exchange(after(solved[1], backs[0], sent)))
    near = exchange(after(both_call(side, rad, own[2], sent), backs[1]))
    far = partner(near[:, 1])
    backs.append(exchange(after(radial_call(rad[:2], own[3], other[2]), near)))
    whole = None
    for planes_of, back in zip((*INNER, OUTER[1]), backs):
        whole = place_call(planes_of, back, whole, velocity.shape)
    whole = weave_call(side, OUTER[0], near, far, whole)
    return whole


def solution(mesh):
    placed = (
        P(None, "ax", "rad", None),
        P("ax", "rad", None),
        P("ax"),
        P("rad"),
        P("rad"),
        P(),
        P(),
    )
    return jax.shard_map(
        local, mesh=mesh, in_specs=placed, out_specs=P(None, "ax", "rad", None), check_vma=False
    )
```

```python
import functools

import jax
import jax.numpy as jnp
from jax import lax
from jax.experimental import pallas as pl
from jax.experimental.pallas import tpu as pltpu
from jax.sharding import PartitionSpec as P

COEF = 0.25
F32 = jnp.float32
BF16 = jnp.bfloat16
INNER = ((2, 3), (4, 5))
OUTER = ((0, 1), (6, 7))
HALF_BYTES = 200 * 1024 * 1024
COLUMNS = 512
VMEM_LIMIT = 56 * 1024 * 1024


def split(x):
    hi = x.astype(BF16)
    return hi, (x - hi.astype(F32)).astype(BF16)


def dot3(a_hi, a_lo, b_hi, b_lo, dims):
    dot = functools.partial(
        lax.dot_general, dimension_numbers=(dims, ((), ())), preferred_element_type=F32
    )
    return dot(a_hi, b_hi) + (dot(a_hi, b_lo) + dot(a_lo, b_hi))


def split_kernel(x_ref, hi_ref, lo_ref):
    hi_ref[...], lo_ref[...] = split(x_ref[...].T)


def split_call(x):
    rows, cols = x.shape
    spec = pl.BlockSpec((256, cols), lambda i: (i, 0))
    return pl.pallas_call(
        split_kernel,
        name=f"split_{rows}",
        grid=(rows // 256,),
        in_specs=[spec],
        out_specs=[pl.BlockSpec((cols, 256), lambda i: (0, i))] * 2,
        out_shape=[jax.ShapeDtypeStruct((cols, rows), BF16)] * 2,
    )(x)


def rhs_kernel(
    groups, edge, inv_dx, inv_dr, inv_rt, velocity, viscosity, rad_lo, rad_hi, *rest
):
    if edge:
        ax_lo, ax_hi, az_hi, az_lo, *outs = rest
    else:
        az_hi, az_lo, *outs = rest
    *outs, vbuf, nbuf, rhs, hi, lo, sems = outs
    planes, rows, nt = viscosity.shape
    width = outs[0].shape[3]
    copies = []

    def bring(source, target):
        copy = pltpu.make_async_copy(source, target, sems.at[len(copies)])
        copy.start()
        copies.append(copy)

    chosen = [p for group in groups for p in group]
    first, last = max(min(chosen) - 2, 0), min(max(chosen) + 3, planes)
    inner, mine = pl.ds(8, rows), pl.ds(first, last - first)
    held = pl.ds(first + 2, last - first)
    for c in range(3):
        bring(velocity.at[c, mine], vbuf.at[c, held, inner])
    bring(viscosity.at[mine], nbuf.at[held, inner])
    if edge:
        for halo, at, thin in ((ax_lo, 0, 1), (ax_hi, planes + 2, planes + 2)):
            for c in range(3):
                bring(halo.at[pl.ds(2 * c, 2)], vbuf.at[c, pl.ds(at, 2), inner])
            bring(halo.at[6], nbuf.at[thin, inner])
    for copy in copies:
        copy.wait()

    def stencil(place, p):
        at = p + 2
        low, high = rad_lo[p], rad_hi[p]
        for c in range(3):
            vbuf[c, at, 0:8, :] = pltpu.roll(low, 6 - 2 * c, 0)
            vbuf[c, at, rows + 8 : rows + 16, :] = pltpu.roll(high, (8 - 2 * c) % 8, 0)
        nbuf[at, 0:8, :] = pltpu.roll(low, 1, 0)
        nbuf[at, rows + 8 : rows + 16, :] = pltpu.roll(high, 2, 0)
        gx = inv_dx[p]

        def strip(i, carry):
            r0 = pl.multiple_of(i * 8, 8)
            mid = pl.ds(pl.multiple_of(r0 + 8, 8), 8)
            wide = pl.ds(r0, 24)
            metrics = (gx, inv_rt[pl.ds(r0, 8), :], inv_dr[pl.ds(r0, 8), :])
            metrics = tuple(
                (g, (0.5 * COEF) * g * g, (COEF / 12.0) * g) for g in metrics
            )
            for l0 in range(0, nt, COLUMNS):
                cols = pl.ds(l0, COLUMNS)
                before, behind = pl.ds((l0 - 128) % nt, 128), pl.ds((l0 + COLUMNS) % nt, 128)

                def turned(ref, *shifts):
                    ext = jnp.concatenate(
                        [ref[mid, before], ref[mid, cols], ref[mid, behind]], axis=1
                    )
                    size = COLUMNS + 256
                    return [
                        pltpu.roll(ext, shift % size, 1)[:, 128 : 128 + COLUMNS]
                        for shift in shifts
                    ]

                nu24 = nbuf[at, wide, cols]
                nu = nu24[8:16]
                nus = (
                    (nbuf[at + 1, mid, cols], nbuf[at - 1, mid, cols]),
                    turned(nbuf.at[at], -1, 1),
                    (nu24[9:17], nu24[7:15]),
                )
                coefs = []
                centre = None
                for d, ((up, down), (_, gg, g12)) in enumerate(zip(nus, metrics)):
                    a_up = gg * (nu + up)
                    a_down = gg * (nu + down)
                    b = g12 * vbuf[d, at, mid, cols]
                    b8 = 8.0 * b
                    total = a_up + a_down
                    centre = total if centre is None else centre + total
                    coefs.append((a_up - b8, a_down + b8, b))
                centre = 1.0 - centre
                for c in range(3):
                    q24 = vbuf[c, at, wide, cols]
                    near = (
                        [vbuf[c, at + k, mid, cols] for k in (1, -1, 2, -2)],
                        turned(vbuf.at[c, at], -1, 1, -2, 2),
                        [q24[8 + k : 16 + k] for k in (1, -1, 2, -2)],
                    )
                    total = centre * q24[8:16]
                    for (up, down, up2, down2), (c_up, c_down, b) in zip(near, coefs):
                        total = total + (c_up * up + c_down * down + b * (up2 - down2))
                    rhs[place, c, pl.ds(r0, 8), cols] = total
            return carry

        lax.fori_loop(0, rows // 8, strip, 0)

    for group, out in zip(groups, outs):
        size = len(group)

        low = sum(p < group[0] + len(group) for p in group)
        jump = group[-1] - group[0] - size + 1

        def plane(j, carry):
            stencil(j, group[0] + j + jnp.where(j >= low, jump, 0))
            return carry

        lax.fori_loop(0, size, plane, 0)
        lines = size * rows
        hi[0 : 3 * lines, :], lo[0 : 3 * lines, :] = split(rhs[0:size].reshape(3 * lines, nt))
        for d in range(nt // width):
            cols = pl.ds(d * width, width)
            solved = dot3(
                hi[0 : 3 * lines, :], lo[0 : 3 * lines, :], az_hi[:, cols], az_lo[:, cols],
                ((1,), (0,)),
            )
            out[d] = solved.reshape(3 * size, rows, width)


def rhs_call(groups, parts, inv_dx, inv_dr, inv_rt, velocity, viscosity, rad_lo, rad_hi, ax, az):
    rows, nt = velocity.shape[2], velocity.shape[3]
    anywhere = pl.BlockSpec(memory_space=pl.ANY)
    vmem = pl.BlockSpec(memory_space=pltpu.VMEM)
    most = max(len(group) for group in groups)
    return pl.pallas_call(
        functools.partial(rhs_kernel, groups, bool(ax)),
        name=f"rhs_{groups[0][0]}",
        in_specs=[pl.BlockSpec(memory_space=pltpu.SMEM), vmem, vmem, anywhere, anywhere, vmem, vmem]
        + [anywhere] * len(ax)
        + [vmem, vmem],
        out_specs=[vmem] * len(groups),
        out_shape=[
            jax.ShapeDtypeStruct((parts, 3 * len(group), rows, nt // parts), F32)
            for group in groups
        ],
        scratch_shapes=[
            pltpu.VMEM((3, 12, rows + 16, nt), F32),
            pltpu.VMEM((12, rows + 16, nt), F32),
            pltpu.VMEM((most, 3, rows, nt), F32),
            pltpu.VMEM((3 * most * rows, nt), BF16),
            pltpu.VMEM((3 * most * rows, nt), BF16),
            pltpu.SemaphoreType.DMA((12,)),
        ],
        compiler_params=pltpu.CompilerParams(vmem_limit_bytes=VMEM_LIMIT),
        cost_estimate=pl.CostEstimate(flops=1024, bytes_accessed=1024, transcendentals=0),
    )(inv_dx, inv_dr[:, None], inv_rt[:, None], velocity, viscosity, rad_lo, rad_hi, *ax, *az)


def half_kernel(side_ref, x_ref, hi_ref, lo_ref, hi_far_ref, lo_far_ref):
    rows = x_ref.shape[0] // 8
    side = side_ref[0]
    for part in range(4):
        at = slice(part * rows, (part + 1) * rows)
        for one, hi, lo in ((side, hi_ref, lo_ref), (1 - side, hi_far_ref, lo_far_ref)):
            x = x_ref[pl.ds(pl.multiple_of(part * 2 * rows + one * rows, rows), rows), :]
            swapped = jnp.concatenate(
                [
                    pltpu.roll(x[:, low : low + 2 * rows], rows, 1)
                    for low in range(0, x.shape[1], 2 * rows)
                ],
                axis=1,
            )
            hi[at, :], lo[at, :] = split(jnp.where(side == 0, x, swapped))


def half_call(side, x):
    rows, cols = x.shape
    vmem = pl.BlockSpec(memory_space=pltpu.VMEM)
    return pl.pallas_call(
        half_kernel,
        name="half",
        in_specs=[pl.BlockSpec(memory_space=pltpu.SMEM), vmem],
        out_specs=[vmem] * 4,
        out_shape=[jax.ShapeDtypeStruct((rows // 2, cols), BF16)] * 4,
    )(side, x)


def radial_kernel(r_hi, r_lo, own_ref, *rest):
    *others, out_ref = rest
    parts, slabs, rows, width = own_ref.shape
    theirs = [(ref, part) for ref in others for part in range(ref.shape[0])]
    x = jnp.concatenate(
        [
            jnp.concatenate(
                [
                    ref[at, s]
                    for part in range(parts)
                    for ref, at in ((own_ref, part), theirs[part])
                ],
                axis=0,
            )
            for s in range(slabs)
        ],
        axis=1,
    )
    hi, lo = split(x)
    y = dot3(r_hi[...], r_lo[...], hi, lo, ((1,), (0,)))
    for s in range(slabs):
        out_ref[:, s] = y[:, s * width : (s + 1) * width].reshape(parts, rows, width)


def radial_call(rad, own, others):
    parts, slabs, rows, width = own.shape

    def block(x):
        return pl.BlockSpec((x.shape[0], 3, rows, width), lambda i: (0, i, 0, 0))

    full = pl.BlockSpec(rad[0].shape, lambda i: (0, 0))
    return pl.pallas_call(
        radial_kernel,
        name="radial",
        grid=(slabs // 3,),
        in_specs=[full, full, block(own)] + [block(x) for x in others],
        out_specs=block(own),
        out_shape=jax.ShapeDtypeStruct(own.shape, F32),
        compiler_params=pltpu.CompilerParams(vmem_limit_bytes=VMEM_LIMIT),
        cost_estimate=pl.CostEstimate(flops=1024, bytes_accessed=1024, transcendentals=0),
    )(*rad, own, *others)


def both_kernel(side_ref, r_hi, r_lo, f_hi, f_lo, own_ref, other_ref, out_ref):
    parts, slabs, rows, width = other_ref.shape
    mine = pl.ds(pl.multiple_of(side_ref[0] * width, width), width)
    x = jnp.concatenate(
        [
            jnp.concatenate(
                [
                    piece
                    for part in range(parts)
                    for piece in (own_ref[part, s, :, mine], other_ref[part, s])
                ],
                axis=0,
            )
            for s in range(slabs)
        ],
        axis=1,
    )
    hi, lo = split(x)
    for way, (a_hi, a_lo) in enumerate(((r_hi, r_lo), (f_hi, f_lo))):
        y = dot3(a_hi[...], a_lo[...], hi, lo, ((1,), (0,)))
        for s in range(slabs):
            out_ref[:, way, s] = y[:, s * width : (s + 1) * width].reshape(parts, rows, width)


def both_call(side, rad, own, other):
    parts, slabs, rows, width = other.shape
    full = pl.BlockSpec(rad[0].shape, lambda i: (0, 0))
    return pl.pallas_call(
        both_kernel,
        name="radial_both",
        grid=(slabs // 3,),
        in_specs=[pl.BlockSpec(memory_space=pltpu.SMEM)]
        + [full] * 4
        + [
            pl.BlockSpec((parts, 3, rows, 2 * width), lambda i: (0, i, 0, 0)),
            pl.BlockSpec((parts, 3, rows, width), lambda i: (0, i, 0, 0)),
        ],
        out_specs=pl.BlockSpec((parts, 2, 3, rows, width), lambda i: (0, 0, i, 0, 0)),
        out_shape=jax.ShapeDtypeStruct((parts, 2, slabs, rows, width), F32),
        compiler_params=pltpu.CompilerParams(vmem_limit_bytes=VMEM_LIMIT),
        cost_estimate=pl.CostEstimate(flops=1024, bytes_accessed=1024, transcendentals=0),
    )(side, *rad, own, other)


def weave_kernel(side_ref, near_ref, far_ref, _, out_ref):
    parts, _, _, _, width = near_ref.shape
    side = side_ref[0]
    for d in range(parts):
        for c in range(3):
            for at, value in ((side, near_ref[d, 0, c]), (1 - side, far_ref[d, c])):
                cols = pl.ds(pl.multiple_of((2 * d + at) * width, width), width)
                out_ref[c, 0, :, cols] = value


def weave_call(side, planes, near, far, whole):
    parts, _, rows, width = far.shape
    first = planes[0]
    return pl.pallas_call(
        weave_kernel,
        name="weave",
        grid=(len(planes),),
        in_specs=[
            pl.BlockSpec(memory_space=pltpu.SMEM),
            pl.BlockSpec((parts, 1, 3, rows, width), lambda j: (0, 0, j, 0, 0)),
            pl.BlockSpec((parts, 3, rows, width), lambda j: (0, j, 0, 0)),
            pl.BlockSpec(memory_space=pl.ANY),
        ],
        out_specs=pl.BlockSpec((3, 1, rows, 2 * parts * width), lambda j: (0, first + j, 0, 0)),
        out_shape=jax.ShapeDtypeStruct(whole.shape, F32),
        input_output_aliases={3: 0},
        cost_estimate=pl.CostEstimate(flops=0, bytes_accessed=16 * far.size, transcendentals=0),
    )(side, near, far, whole)


def place_kernel(x_ref, *rest):
    out_ref = rest[-1]
    parts, width = x_ref.shape[0], x_ref.shape[3]
    for d in range(parts):
        for c in range(3):
            out_ref[c, 0, :, d * width : (d + 1) * width] = x_ref[d, c]


def place_call(planes, x, whole, shape):
    parts, _, rows, width = x.shape
    first = planes[0]
    aliased = () if whole is None else (whole,)
    return pl.pallas_call(
        place_kernel,
        name="place",
        grid=(len(planes),),
        in_specs=[pl.BlockSpec((parts, 3, rows, width), lambda j: (0, j, 0, 0))]
        + [pl.BlockSpec(memory_space=pl.ANY)] * len(aliased),
        out_specs=pl.BlockSpec((3, 1, rows, parts * width), lambda j: (0, first + j, 0, 0)),
        out_shape=jax.ShapeDtypeStruct(shape, F32),
        input_output_aliases={1: 0} if aliased else {},
        cost_estimate=pl.CostEstimate(flops=0, bytes_accessed=8 * x.size, transcendentals=0),
    )(x, *aliased)


def line_kernel(velocity, viscosity, top, bottom, edges, sems):
    planes, rows = viscosity.shape[0], viscosity.shape[1]
    copies = []
    for side, at in enumerate((rows - 8, 0)):
        for f in range(4):
            source = velocity.at[f, :, pl.ds(at, 8)] if f < 3 else viscosity.at[:, pl.ds(at, 8)]
            copies.append(
                pltpu.make_async_copy(source, edges.at[side, f], sems.at[len(copies)])
            )
    for copy in copies:
        copy.start()
    for copy in copies:
        copy.wait()
    row = lax.broadcasted_iota(jnp.int32, edges.shape[3:], 0)
    for p in range(planes):
        for side, out, turns in ((0, top, (2, 4, 6, 7)), (1, bottom, (0, 2, 4, 6))):
            strips = [
                pltpu.roll(edges[side, f, p], turn, 0) if turn else edges[side, f, p]
                for f, turn in enumerate(turns)
            ]
            out[p] = jnp.where(
                row < 4,
                jnp.where(row < 2, strips[0], strips[1]),
                jnp.where(row < 6, strips[2], strips[3]),
            )


def line_call(velocity, viscosity):
    planes, _, nt = viscosity.shape
    anywhere = pl.BlockSpec(memory_space=pl.ANY)
    vmem = pl.BlockSpec(memory_space=pltpu.VMEM)
    return pl.pallas_call(
        line_kernel,
        name="lines",
        in_specs=[anywhere, anywhere],
        out_specs=[vmem, vmem],
        out_shape=[jax.ShapeDtypeStruct((planes, 8, nt), F32)] * 2,
        scratch_shapes=[pltpu.VMEM((2, 4, planes, 8, nt), F32), pltpu.SemaphoreType.DMA((8,))],
        compiler_params=pltpu.CompilerParams(vmem_limit_bytes=VMEM_LIMIT),
    )(velocity, viscosity)


def face_kernel(velocity, viscosity, top, bottom, sems):
    planes = viscosity.shape[0]
    copies = []
    for out, at, thin in ((top, planes - 2, planes - 1), (bottom, 0, 0)):
        for f in range(4):
            source = velocity.at[f, pl.ds(at, 2)] if f < 3 else viscosity.at[pl.ds(thin, 1)]
            target = out.at[pl.ds(2 * f, 2 if f < 3 else 1)]
            copies.append(pltpu.make_async_copy(source, target, sems.at[len(copies)]))
    for copy in copies:
        copy.start()
    for copy in copies:
        copy.wait()


def face_call(velocity, viscosity):
    _, rows, nt = viscosity.shape
    anywhere = pl.BlockSpec(memory_space=pl.ANY)
    vmem = pl.BlockSpec(memory_space=pltpu.VMEM)
    return pl.pallas_call(
        face_kernel,
        name="faces",
        in_specs=[anywhere, anywhere],
        out_specs=[vmem, vmem],
        out_shape=[jax.ShapeDtypeStruct((7, rows, nt), F32)] * 2,
        scratch_shapes=[pltpu.SemaphoreType.DMA((8,))],
        compiler_params=pltpu.CompilerParams(vmem_limit_bytes=VMEM_LIMIT),
    )(velocity, viscosity)


def after(x, *events):
    return lax.optimization_barrier((x, *events))[0]


def local(velocity, viscosity, inv_dx, inv_dr, inv_rt, az_inverse, rad_inverse):
    planes = velocity.shape[1]
    lines = lax.axis_size("rad")
    parts = lines // 2
    side = (lax.axis_index("rad") % 2).astype(jnp.int32).reshape(1)

    def shifts(axis):
        count = lax.axis_size(axis)
        forward = [(i, i + 1) for i in range(count - 1)]
        return forward, [(b, a) for a, b in forward]

    rad_top, rad_bottom = line_call(velocity, viscosity)
    forward, backward = shifts("rad")
    rad_lo = lax.ppermute(rad_top, "rad", forward)
    rad_hi = lax.ppermute(rad_bottom, "rad", backward)
    ax_top, ax_bottom = face_call(velocity, after(viscosity, rad_top))
    az = split_call(after(az_inverse, ax_top))
    forward, backward = shifts("ax")
    ax_top, ax_bottom, rad_lo, rad_hi, *_ = lax.optimization_barrier(
        (ax_top, ax_bottom, rad_lo, rad_hi, az[0])
    )
    ax_lo = lax.ppermute(ax_top, "ax", forward)
    ax_hi = lax.ppermute(ax_bottom, "ax", backward)
    groups = [list(range(0, lines, 2)), list(range(1, lines, 2))]

    def exchange(x):
        return lax.all_to_all(
            x, "rad", split_axis=0, concat_axis=0, tiled=True, axis_index_groups=groups
        )

    def partner(x):
        return lax.ppermute(x, "rad", [(i, i ^ 1) for i in range(lines)])

    common = (inv_dr, inv_rt, velocity, viscosity, rad_lo, rad_hi)
    (first,) = rhs_call(INNER[:1], parts, inv_dx, *common, (), az)
    rad = half_call(after(side, first), rad_inverse)
    (second,) = rhs_call(INNER[1:], parts, after(inv_dx, first, rad[0]), *common, (), az)
    second, ax_lo, ax_hi = lax.optimization_barrier((second, ax_lo, ax_hi))
    own = [exchange(first)]
    other = [(partner(after(own[0], ax_lo)),)]
    own.append(exchange(after(second, own[0])))
    dx, faces = after(inv_dx, own[0]), (ax_lo, ax_hi)
    edges = rhs_call(OUTER[:1], parts, dx, *common, faces, az)
    edges += rhs_call(OUTER[1:], parts, after(dx, edges[0], own[1]), *common, faces, az)
    own.append(exchange(after(edges[0], own[1])))
    other.append((partner(after(own[1], edges[0])),))
    solved = [radial_call(rad[:2], own[k], other[k]) for k in range(2)]
    own.append(exchange(after(edges[1], own[2], solved[0])))
    width = own[2].shape[3] // 2
    sent = lax.dynamic_slice_in_dim(own[2], (1 - side[0]) * width, width, axis=3)
    sent = partner(after(sent, other[0][0]))
    other.append((partner(after(own[3], other[1][0])),))
    backs = [exchange(after(solved[0], own[3], other[1][0]))]
    backs.append(exchange(after(solved[1], backs[0], sent)))
    near = exchange(after(both_call(side, rad, own[2], sent), backs[1]))
    far = partner(near[:, 1])
    backs.append(exchange(after(radial_call(rad[:2], own[3], other[2]), near)))
    whole = None
    for planes_of, back in zip((*INNER, OUTER[1]), backs):
        whole = place_call(planes_of, back, whole, velocity.shape)
    whole = weave_call(side, OUTER[0], near, far, whole)
    return whole


def solution(mesh):
    placed = (
        P(None, "ax", "rad", None),
        P("ax", "rad", None),
        P("ax"),
        P("rad"),
        P("rad"),
        P(),
        P(),
    )
    return jax.shard_map(
        local, mesh=mesh, in_specs=placed, out_specs=P(None, "ax", "rad", None), check_vma=False
    )
```
